32 devices in a mesh: group: 4 (over x, core), replica: 8 (over z, y).
Axes of the slice: x: 2, y: 2, z: 4, core: 2. Of those that a mesh axis runs over, the one named last changes fastest.
Arguments:
- tokens: bfloat16 [8, 512, 768], P('replica', 'group'), may hold values from -6 to 6
- segment_ids: int32 [8, 512], P('replica'), may hold values from 0 to 3, as said below
- cotangent: bfloat16 [8, 512, 768], P('replica', 'group'), may hold values from -6 to 6
- qkv_weight: bfloat16 [768, 2304], P('group'), may hold values from -0.21875 to 0.21875
- qv_bias: bfloat16 [1536], P('group'), may hold values from -3 to 3
- out_weight: bfloat16 [768, 768], P('group'), may hold values from -0.625 to 0.625
- out_bias: bfloat16 [768], P('group'), may hold values from -3 to 3
- norm1_gain: bfloat16 [768], P('group'), may hold values from 0.099609375 to 1.8984375
- norm1_shift: bfloat16 [768], P('group'), may hold values from -3 to 3
- up_weight: bfloat16 [768, 3072], P('group'), may hold values from -0.21875 to 0.21875
- up_bias: bfloat16 [3072], P('group'), may hold values from -3 to 3
- down_weight: bfloat16 [3072, 768], P('group'), may hold values from -0.15625 to 0.15625
- down_bias: bfloat16 [768], P('group'), may hold values from -3 to 3
- norm2_gain: bfloat16 [768], P('group'), may hold values from 0.099609375 to 1.8984375
- norm2_shift: bfloat16 [768], P('group'), may hold values from -3 to 3
Outputs:
- output: bfloat16 [8, 512, 768], P('replica', 'group')
- grad_tokens: bfloat16 [8, 512, 768], P('replica', 'group')
- grad_qkv_weight: float32 [768, 2304], P('group')
- grad_qv_bias: float32 [1536], P('group')
- grad_out_weight: float32 [768, 768], P('group')
- grad_out_bias: float32 [768], P('group')
- grad_norm1_gain: float32 [768], P('group')
- grad_norm1_shift: float32 [768], P('group')
- grad_up_weight: float32 [768, 3072], P('group')
- grad_up_bias: float32 [3072], P('group')
- grad_down_weight: float32 [3072, 768], P('group')
- grad_down_bias: float32 [768], P('group')
- grad_norm2_gain: float32 [768], P('group')
- grad_norm2_shift: float32 [768], P('group')
The draws below stay inside these ranges and needn't reach their ends.
Inputs may be any that keep to these rules, and one draw needn't show every extreme that they name: `segment_ids`: within each sequence the numbers never fall; in every sequence one document starts within the first 64 positions and ends within the last 64.
All inputs are finite; a program needn't handle non-finite values.
Results may differ from the reference program's by a relative error of at most 0.018.
Values may be sent and summed in bfloat16 or wider, within the bound.
No kernel may reach another device: no remote copies, remote signals or barrier semaphores. Data moves between devices by JAX's collectives and lax.ppermute only.
A program may use at most 128 MiB of HBM per device.

```python
import math
import jax
import jax.numpy as jnp
from jax import lax

D = 768
H = 12
HD = 64
FF = 3072
LEN = 512
SEQS = 8


def draw_segment_ids(key, part):
    key = jax.random.fold_in(key, 7)
    first_key, last_key, extra_key = jax.random.split(key, 3)
    edge = LEN // 8
    opening = jax.random.randint(first_key, (SEQS, 1), 1, edge)
    closing = jax.random.randint(last_key, (SEQS, 1), LEN - edge, LEN)
    further = jax.random.randint(extra_key, (SEQS, 1), 1, edge)
    places = jnp.arange(LEN, dtype=jnp.int32)[None, :]
    return (places >= opening).astype(jnp.int32) + (places >= closing).astype(jnp.int32) + (places >= further).astype(jnp.int32)


def levels(own_key, dims, shards, least, top_value):
    loudness = 1.0
    for dim, shards_of in shards:
        heights = jax.random.uniform(jax.random.fold_in(jax.random.fold_in(own_key, 6), dim), (shards_of,), jnp.float32, least / len(shards), top_value / len(shards))
        loudness = loudness * jnp.repeat(jnp.exp(heights), dims[dim] // shards_of).reshape((-1,) + (1,) * (len(dims) - 1 - dim))
    return loudness


def centred(stream_key, dims, scale, bound, pieces=(), kind=jnp.bfloat16):
    factor_of = levels(stream_key, dims, pieces, -0.22, 0.18) if pieces else 1.0
    values = jax.random.normal(stream_key, dims, jnp.float32) * scale * factor_of
    return jnp.minimum(jnp.maximum(values, -bound), bound).astype(kind)


def setup_inputs(seed: int = 0) -> dict:
    seeds = jax.random.split(jax.random.key(seed), 16)
    return {
        "tokens": centred(seeds[0], (SEQS, LEN, D), 1.0, 6.0, ((0, 8), (1, 4))),
        "segment_ids": draw_segment_ids(jax.random.fold_in(seeds[15], 71), 0),
        "cotangent": centred(seeds[2], (SEQS, LEN, D), 1.0, 6.0, ((0, 8), (1, 4))),
        "qkv_weight": centred(seeds[3], (D, 3 * D), D ** -0.5, 0.21875, ((0, 4),)),
        "qv_bias": centred(seeds[4], (2 * D,), 0.5, 3.0, ((0, 4),)),
        "out_weight": centred(seeds[5], (D, D), (D // 8) ** -0.5, 0.625, ((0, 4),)),
        "out_bias": centred(seeds[6], (D,), 0.4, 3.0, ((0, 4),)),
        "norm1_gain": jnp.clip(1.0 + 0.18 * jax.random.normal(seeds[7], (D,), jnp.float32), 0.099609375, 1.8984375).astype(jnp.bfloat16),
        "norm1_shift": centred(seeds[8], (D,), 0.5, 3.0, ((0, 4),)),
        "up_weight": centred(seeds[9], (D, FF), D ** -0.5, 0.21875, ((0, 4),)),
        "up_bias": centred(seeds[10], (FF,), 0.5, 3.0, ((0, 4),)),
        "down_weight": centred(seeds[11], (FF, D), (FF // 2) ** -0.5, 0.15625, ((0, 4),)),
        "down_bias": centred(seeds[12], (D,), 0.4, 3.0, ((0, 4),)),
        "norm2_gain": jnp.clip(1.0 + 0.18 * jax.random.normal(seeds[13], (D,), jnp.float32), 0.099609375, 1.8984375).astype(jnp.bfloat16),
        "norm2_shift": centred(seeds[14], (D,), 0.5, 3.0, ((0, 4),)),
    }


@jax.custom_vjp
def low(v):
    return lax.optimization_barrier(v.astype(jnp.bfloat16)).astype(jnp.float32)

@jax.custom_vjp
def low_back(v):
    return v

def low_keep(v):
    return (low(v), None)

def low_pass(kept, grad):
    return (grad,)

def back_keep(v):
    return (v, None)

def back_low(kept, grad):
    return (low(grad),)
low.defvjp(low_keep, low_pass)
low_back.defvjp(back_keep, back_low)
EPS = 1e-05

def norm_apply(value, gain, shift):
    centre = value - lax.optimization_barrier(jnp.mean(value, axis=-1, keepdims=True))
    spread = lax.optimization_barrier(jnp.mean(centre * centre, axis=-1, keepdims=True))
    return centre * lax.rsqrt(spread + EPS) * gain + shift

def forward(inputs, segments, params):
    qkv_weight, qv_bias, out_weight, out_bias, gain_one, shift_one, up_weight, up_bias, down_weight, down_bias, gain_two, shift_two = params
    highest = lax.Precision.HIGHEST
    count = inputs.shape[0]
    bias_full = jnp.concatenate([qv_bias[:D], jnp.zeros((D,), jnp.float32), qv_bias[D:]])
    proj = low_back(low(jnp.einsum('bld,de->ble', inputs, qkv_weight, precision=highest) + bias_full))
    queries = proj[..., :D].reshape(count, LEN, H, HD)
    keys = proj[..., D:2 * D].reshape(count, LEN, H, HD)
    values = proj[..., 2 * D:].reshape(count, LEN, H, HD)
    scores = low_back(jnp.einsum('bqhd,bkhd->bhqk', queries, keys, precision=highest) * HD ** (-0.5))
    same = segments[:, None, :, None] == segments[:, None, None, :]
    scores = jnp.where(same, scores, jnp.float32(-1e+30))
    probs = low(jax.nn.softmax(scores, axis=-1))
    attended = jnp.einsum('bhqk,bkhd->bqhd', probs, values, precision=highest).reshape(count, LEN, D)
    attended = low_back(low(attended))
    branch = low_back(jnp.einsum('bld,de->ble', attended, out_weight, precision=highest) + out_bias)
    normed = norm_apply(inputs + branch, gain_one, shift_one)
    pre = low_back(jnp.einsum('bld,df->blf', low(normed), up_weight, precision=highest) + up_bias)
    act = low(jax.nn.gelu(pre, approximate=False))
    second = low_back(jnp.einsum('blf,fd->bld', act, down_weight, precision=highest) + down_bias)
    return norm_apply(normed + second, gain_two, shift_two)

def reference(tokens, segment_ids, cotangent, qkv_weight, qv_bias, out_weight, out_bias, norm1_gain, norm1_shift, up_weight, up_bias, down_weight, down_bias, norm2_gain, norm2_shift):
    params = tuple((p.astype(jnp.float32) for p in (qkv_weight, qv_bias, out_weight, out_bias, norm1_gain, norm1_shift, up_weight, up_bias, down_weight, down_bias, norm2_gain, norm2_shift)))
    blocksize = math.gcd(SEQS, 8)
    blocks = SEQS // blocksize
    inputs = tokens.astype(jnp.float32).reshape(blocks, blocksize, LEN, D)
    segments = segment_ids.reshape(blocks, blocksize, LEN)
    upstream = cotangent.astype(jnp.float32).reshape(blocks, blocksize, LEN, D)

    def step(totals, item):
        block_in, block_seg, block_up = item
        result, pullback = jax.vjp(lambda a, b: forward(a, block_seg, b), block_in, params)
        grad_in, grad_params = pullback(block_up)
        totals = jax.tree.map(lambda s, t: s + t, totals, grad_params)
        return (totals, (result.astype(jnp.bfloat16), grad_in.astype(jnp.bfloat16)))
    start = jax.tree.map(jnp.zeros_like, params)
    totals, (results, grads_in) = lax.scan(step, start, (inputs, segments, upstream))
    return (results.reshape(SEQS, LEN, D), grads_in.reshape(SEQS, LEN, D), totals[0], totals[1], totals[2], totals[3], totals[4], totals[5], totals[6], totals[7], totals[8], totals[9], totals[10], totals[11])
```

```python
from functools import partial

import jax
import jax.numpy as jnp
from jax import lax
from jax.sharding import PartitionSpec as P

HD = 64
G = 4
EPS = 1e-05
BF = jnp.bfloat16
F32 = jnp.float32


def gx(value, bits):
    return lax.ppermute(value, "group", [(i, i ^ bits) for i in range(G)])


def rx(value, bits, count):
    return lax.ppermute(value, "replica", [(i, i ^ bits) for i in range(count)])


def dot(a, b):
    return jnp.dot(a, b, preferred_element_type=F32)


def dot_t(a, b):
    return lax.dot_general(a, b, (((1,), (1,)), ((), ())), preferred_element_type=F32)


def t_dot(a, b):
    return lax.dot_general(a, b, (((0,), (0,)), ((), ())), preferred_element_type=F32)


def xor_order(items, place):
    count = len(items)
    bit = 1
    while bit < count:
        on = (place & bit) != 0
        items = [jnp.where(on, items[i ^ bit], items[i]) for i in range(count)]
        bit *= 2
    return items


def gather_rows(own):
    far = gx(own, 2)
    near = gx(own, 1)
    return own, near, far, gx(far, 1)


def scatter_rows(parts):
    far = parts[2] + gx(parts[3].astype(BF), 1).astype(F32)
    far = gx(far.astype(BF), 2)
    near = gx(parts[1].astype(BF), 1)
    return parts[0] + near.astype(F32) + far.astype(F32)


def replica_scatter(value, order, me, count):
    top = count.bit_length() - 1
    rest = value.shape[1:]
    value = value.reshape((2,) * top + rest)
    left = list(range(top - 1, -1, -1))
    for bit in order:
        axis = left.index(bit)
        mine = (me >> bit) & 1
        other = lax.dynamic_index_in_dim(value, 1 - mine, axis, keepdims=False)
        keep = lax.dynamic_index_in_dim(value, mine, axis, keepdims=False)
        got = rx(other, 1 << bit, count)
        value = (keep.astype(F32) + got.astype(F32)).astype(BF)
        left.remove(bit)
    return value


def replica_gather(value, order, me, count):
    top = count.bit_length() - 1
    rest = value.shape
    left = []
    for bit in reversed(order):
        got = rx(value, 1 << bit, count)
        on = ((me >> bit) & 1) != 0
        left = sorted(left + [bit], reverse=True)
        axis = left.index(bit)
        value = jnp.stack([jnp.where(on, got, value), jnp.where(on, value, got)], axis=axis)
    return value.reshape((count,) + rest)


def norm_parts(value):
    centre = value - jnp.mean(value, axis=-1, keepdims=True)
    spread = jnp.mean(centre * centre, axis=-1, keepdims=True)
    scale = lax.rsqrt(spread + EPS)
    return centre * scale, scale


def norm_back(upstream, hat, scale, gain):
    scaled = upstream * gain
    first = jnp.mean(scaled, axis=-1, keepdims=True)
    second = jnp.mean(scaled * hat, axis=-1, keepdims=True)
    return scale * (scaled - first - hat * second)


def on_device(
    replicas,
    tokens,
    segment_ids,
    cotangent,
    qkv_weight,
    qv_bias,
    out_weight,
    out_bias,
    norm1_gain,
    norm1_shift,
    up_weight,
    up_bias,
    down_weight,
    down_bias,
    norm2_gain,
    norm2_shift,
):
    place = lax.axis_index("group")
    me = lax.axis_index("replica")
    rows, width = tokens.shape[1], tokens.shape[2]
    part = width // G
    hidden = up_weight.shape[1] // G
    heads = part // HD
    bits = list(range(replicas.bit_length() - 1))
    order_a = bits
    order_b = bits[1:] + bits[:1]

    own_x = tokens[0]
    x_blocks = gather_rows(own_x)
    qkv_by_dest = qkv_weight.reshape(part, 3, G, part)
    qkv_rows = [
        lax.dynamic_index_in_dim(qkv_by_dest, place ^ k, 2, keepdims=False).reshape(part, 3 * part)
        for k in range(G)
    ]
    qkv_rows = [qkv_rows[0]] + [gx(qkv_rows[k], k) for k in range(1, G)]
    small = jnp.concatenate(
        [qv_bias, out_bias, norm1_gain, norm1_shift, down_bias, norm2_gain, norm2_shift]
    ).reshape(1, -1)
    small = jnp.concatenate(xor_order(list(gather_rows(small)), place), axis=0).astype(F32)
    qv = small[:, : 2 * part].reshape(2, width)
    vectors = small[:, 2 * part :].reshape(G, 6, part).transpose(1, 0, 2).reshape(6, width)
    out_b, gain1, shift1, down_b, gain2, shift2 = [vectors[i] for i in range(6)]
    up_rows = [
        lax.dynamic_slice_in_dim(up_weight, (place ^ k) * hidden, hidden, 1) for k in range(G)
    ]
    up_rows = [up_rows[0]] + [gx(up_rows[k], k) for k in range(1, G)]
    up_bias = up_bias.astype(F32)

    qkv_local = jnp.concatenate(xor_order(qkv_rows, place), axis=0)
    up_local = jnp.concatenate(xor_order(up_rows, place), axis=0)
    own_qv = lax.dynamic_slice_in_dim(qv, place * part, part, 1)
    bias = jnp.concatenate([own_qv[0], jnp.zeros((part,), F32), own_qv[1]])
    segs = segment_ids.reshape(G, rows)
    segs = jnp.concatenate(
        [lax.dynamic_index_in_dim(segs, place ^ k, 0, keepdims=False) for k in range(G)]
    )
    same = segs[:, None] == segs[None, :]

    x_all = jnp.concatenate(x_blocks, axis=0)
    proj = (dot(x_all, qkv_local) + bias).astype(BF)
    scale = HD**-0.5
    attended, kept = [], []
    for h in range(heads):
        q = proj[:, h * HD : (h + 1) * HD]
        k = proj[:, part + h * HD : part + (h + 1) * HD]
        v = proj[:, 2 * part + h * HD : 2 * part + (h + 1) * HD]
        scores = jnp.where(same, dot_t(q, k) * scale, jnp.float32(-1e30))
        peak = jnp.max(scores, axis=-1, keepdims=True)
        expo = jnp.exp(scores - peak)
        probs = expo / jnp.sum(expo, axis=-1, keepdims=True)
        low = probs.astype(BF)
        attended.append(dot(low, v).astype(BF))
        kept.append((q, k, v, probs, low))
    attended = jnp.concatenate(attended, axis=1)
    branch = dot(attended, out_weight)
    branch = scatter_rows([branch[k * rows : (k + 1) * rows] for k in range(G)])
    first = own_x.astype(F32) + branch + out_b
    hat1, scale1 = norm_parts(first)
    normed = hat1 * gain1 + shift1
    normed_low = jnp.concatenate(gather_rows(normed.astype(BF)), axis=0)
    pre = dot(normed_low, up_local) + up_bias
    cdf = 0.5 * (1.0 + lax.erf(pre * (0.5**0.5)))
    act = (pre * cdf).astype(BF)
    slope = cdf + pre * jnp.exp(-0.5 * pre * pre) * ((2 * jnp.pi) ** -0.5)
    second = dot(act, down_weight)
    second = scatter_rows([second[k * rows : (k + 1) * rows] for k in range(G)])
    hat2, scale2 = norm_parts(normed + second + down_b)
    output = (hat2 * gain2 + shift2).astype(BF)

    up_stream = cotangent[0].astype(F32)
    d_sum = norm_back(up_stream, hat2, scale2, gain2)
    d_second = d_sum.astype(BF)
    vec_gain2 = jnp.sum(up_stream * hat2, axis=0)
    vec_shift2 = jnp.sum(up_stream, axis=0)
    vec_down = jnp.sum(d_second.astype(F32), axis=0)
    d_second_all = jnp.concatenate(gather_rows(d_second), axis=0)
    grad_down = t_dot(act, d_second_all).astype(BF)
    d_pre = (dot_t(d_second_all, down_weight) * slope).astype(BF)
    vec_up = jnp.sum(d_pre.astype(F32), axis=0)
    grad_up = t_dot(normed_low, d_pre).astype(BF)
    d_normed = dot_t(d_pre, up_local)
    d_normed = d_sum + scatter_rows([d_normed[k * rows : (k + 1) * rows] for k in range(G)])

    down_piece = replica_scatter(grad_down.reshape(replicas, -1, width), order_a, me, replicas)
    grad_down = replica_gather(down_piece, order_a, me, replicas).reshape(hidden, width)
    cut = part // replicas

    def column_grad(value, order):
        columns = value.shape[1]
        pieces = value.reshape(G, replicas, cut, columns).transpose(1, 0, 2, 3)
        mine = replica_scatter(pieces, order, me, replicas)
        mine = [lax.dynamic_index_in_dim(mine, place ^ k, 0, keepdims=False) for k in range(G)]
        mine = [mine[0]] + [gx(mine[k], k) for k in range(1, G)]
        whole = replica_gather(jnp.stack(mine), order, me, replicas)
        whole = xor_order([whole[:, k].reshape(part, columns).astype(F32) for k in range(G)], place)
        return jnp.stack(whole, axis=1)

    grad_up = column_grad(grad_up, order_b).reshape(part, G * hidden)

    d_first = norm_back(d_normed, hat1, scale1, gain1)
    vec_gain1 = jnp.sum(d_normed * hat1, axis=0)
    vec_shift1 = jnp.sum(d_normed, axis=0)
    d_branch = d_first.astype(BF)
    vec_out = jnp.sum(d_branch.astype(F32), axis=0)
    d_branch_all = jnp.concatenate(gather_rows(d_branch), axis=0)
    grad_out = t_dot(attended, d_branch_all).astype(BF)
    out_piece = replica_scatter(grad_out.reshape(replicas, -1, width), order_a, me, replicas)
    grad_out = replica_gather(out_piece, order_a, me, replicas).reshape(part, width)
    d_att = dot_t(d_branch_all, out_weight).astype(BF)
    d_q, d_k, d_v = [], [], []
    for h in range(heads):
        q, k, v, probs, low = kept[h]
        d_o = d_att[:, h * HD : (h + 1) * HD]
        d_probs = dot_t(d_o, v)
        inner = jnp.sum(probs * d_probs, axis=-1, keepdims=True)
        d_scores = (probs * (d_probs - inner)).astype(BF)
        d_q.append((dot(d_scores, k) * scale).astype(BF))
        d_k.append((t_dot(d_scores, q) * scale).astype(BF))
        d_v.append(t_dot(low, d_o).astype(BF))
    d_proj = jnp.concatenate(d_q + d_k + d_v, axis=1)
    sums = jnp.sum(d_proj.astype(F32), axis=0)
    grad_qkv = t_dot(x_all, d_proj).astype(BF)
    half = 3 * part // 2
    grad_qkv = jnp.concatenate(
        [
            column_grad(grad_qkv[:, :half], order_a),
            column_grad(grad_qkv[:, half:], order_b),
        ],
        axis=2,
    )
    grad_qkv = grad_qkv.reshape(part, G, 3, part).transpose(0, 2, 1, 3).reshape(part, 3 * width)
    d_in = dot_t(d_proj, qkv_local)
    d_in = d_first + scatter_rows([d_in[k * rows : (k + 1) * rows] for k in range(G)])
    grad_tokens = d_in.astype(BF)

    vecs = jnp.concatenate(
        [
            jnp.stack([vec_out, vec_gain1, vec_shift1, vec_down, vec_gain2, vec_shift2]).reshape(-1),
            lax.dynamic_update_slice_in_dim(jnp.zeros((G * hidden,), F32), vec_up, place * hidden, 0),
            lax.dynamic_update_slice_in_dim(
                jnp.zeros((3, width), F32), sums.reshape(3, part), place * part, 1
            ).reshape(-1),
        ]
    ).reshape(-1, width)
    for bit in range(2):
        vecs = vecs + gx(vecs, 1 << bit)
    for bit in bits:
        vecs = vecs + rx(vecs, 1 << bit, replicas)
    six = lax.dynamic_slice_in_dim(vecs[:6], place * part, part, 1)
    vec_up = lax.dynamic_slice_in_dim(vecs[6 : 6 + G].reshape(-1), place * hidden, hidden, 0)
    qvs = jnp.concatenate([vecs[6 + G], vecs[8 + G]])
    vec_qv = lax.dynamic_slice_in_dim(qvs, place * 2 * part, 2 * part, 0)
    return (
        output[None],
        grad_tokens[None],
        grad_qkv,
        vec_qv,
        grad_out.astype(F32),
        six[0],
        six[1],
        six[2],
        grad_up,
        vec_up,
        grad_down.astype(F32),
        six[3],
        six[4],
        six[5],
    )


def solution(mesh):
    rows = P("replica", "group", None)
    flat = P("group")
    matrix = P("group", None)
    in_specs = (
        rows,
        P("replica", None),
        rows,
        matrix,
        flat,
        matrix,
        flat,
        flat,
        flat,
        matrix,
        flat,
        matrix,
        flat,
        flat,
        flat,
    )
    out_specs = (
        rows,
        rows,
        matrix,
        flat,
        matrix,
        flat,
        flat,
        flat,
        matrix,
        flat,
        matrix,
        flat,
        flat,
        flat,
    )
    return jax.shard_map(
        partial(on_device, mesh.shape["replica"]),
        mesh=mesh,
        in_specs=in_specs,
        out_specs=out_specs,
        check_vma=False,
    )
```

```python
from functools import partial

import jax
import jax.numpy as jnp
from jax import lax
from jax.experimental import pallas as pl
from jax.experimental.pallas import tpu as pltpu
from jax.sharding import PartitionSpec as P

HD = 64
G = 4
EPS = 1e-05
BF = jnp.bfloat16
F32 = jnp.float32


def gx(value, bits):
    return lax.ppermute(value, "group", [(i, i ^ bits) for i in range(G)])


def rx(value, bits, count):
    return lax.ppermute(value, "replica", [(i, i ^ bits) for i in range(count)])


def dot(a, b):
    return jnp.dot(a, b, preferred_element_type=F32)


def dot_t(a, b):
    return lax.dot_general(a, b, (((1,), (1,)), ((), ())), preferred_element_type=F32)


def t_dot(a, b):
    return lax.dot_general(a, b, (((0,), (0,)), ((), ())), preferred_element_type=F32)


def xor_order(items, place):
    count = len(items)
    bit = 1
    while bit < count:
        on = (place & bit) != 0
        items = [jnp.where(on, items[i ^ bit], items[i]) for i in range(count)]
        bit *= 2
    return items


def gather_rows(own):
    far = gx(own, 2)
    near = gx(own, 1)
    return own, near, far, gx(far, 1)


def scatter_rows(parts):
    far = parts[2] + gx(parts[3].astype(BF), 1).astype(F32)
    far = gx(far.astype(BF), 2)
    near = gx(parts[1].astype(BF), 1)
    return parts[0] + near.astype(F32) + far.astype(F32)


def after(value, *others):
    return lax.optimization_barrier((value, others))[0]


class Scatter:
    def __init__(self, value, order, me, count):
        self.held, self.rows = [(value, 0)], value.shape[1]
        self.left, self.me, self.count = list(order), me, count

    def total(self, side):
        cut = [
            lax.dynamic_slice_in_dim(array, start + side * self.rows, self.rows, 1).astype(F32)
            for array, start in self.held
        ]
        return sum(cut[1:], cut[0])

    def send(self):
        self.rows //= 2
        self.mine = (self.me >> self.left[0]) & 1
        return self.total(1 - self.mine).astype(BF)

    def swap(self, half):
        return rx(half, 1 << self.left.pop(0), self.count)

    def take(self, got):
        moved = [(array, start + self.mine * self.rows) for array, start in self.held]
        self.held = moved + [(got, 0)]

    def step(self, got):
        self.take(got)
        return self.swap(self.send())

    def piece(self, got):
        self.take(got)
        return self.total(0).astype(BF)


class Gather:
    def __init__(self, value, order, me, count):
        self.value, self.left, self.me, self.count = value, list(order), me, count

    def swap(self):
        return rx(self.value, 1 << self.left[-1], self.count)

    def take(self, got):
        on = ((self.me >> self.left.pop()) & 1) != 0
        self.value = jnp.concatenate(
            [jnp.where(on, got, self.value), jnp.where(on, self.value, got)], axis=1
        )

    def step(self, got):
        self.take(got)
        return self.swap()


def whole_spec():
    return pl.BlockSpec(memory_space=pltpu.VMEM)


def index_spec():
    return pl.BlockSpec(memory_space=pltpu.SMEM)


def call(kernel, out_shape, inputs, flops=0):
    single = not isinstance(out_shape, (list, tuple))
    outs = [out_shape] if single else list(out_shape)
    moved = sum(v.size * v.dtype.itemsize for v in list(inputs) + outs)
    got = pl.pallas_call(
        kernel,
        out_shape=outs,
        in_specs=[index_spec()] + [whole_spec()] * (len(inputs) - 1),
        out_specs=[whole_spec()] * len(outs),
        compiler_params=pltpu.CompilerParams(vmem_limit_bytes=48 * 1024 * 1024),
        cost_estimate=pl.CostEstimate(flops=flops, bytes_accessed=moved, transcendentals=0),
    )(*inputs)
    return got[0] if single else got


def pack_kernel(index, weight, *sends):
    part = weight.shape[0]
    for own in range(G):

        @pl.when(index[0] == own)
        def _():
            for k in range(G):
                dest = own ^ k
                for j in range(3):
                    start = (j * G + dest) * part
                    sends[k][:, j * part : (j + 1) * part] = weight[:, start : start + part]


def join_kernel(index, held, got, out):
    rows = held.shape[0]
    mine = index[1]
    out[pl.ds(pl.multiple_of(mine * rows, rows), rows), :] = held[...].astype(F32)
    out[pl.ds(pl.multiple_of((1 - mine) * rows, rows), rows), :] = got[...].astype(F32)


def join_up_kernel(index, held, got, out):
    rows, columns = held.shape[1], held.shape[2]
    mine = index[2]
    for k in range(G):
        where = pl.ds(pl.multiple_of((index[0] ^ k) * columns, columns), columns)
        out[pl.ds(pl.multiple_of(mine * rows, rows), rows), where] = held[k].astype(F32)
        out[pl.ds(pl.multiple_of((1 - mine) * rows, rows), rows), where] = got[k].astype(F32)


def join_tail_kernel(index, held_one, got_one, held_two, got_two, out, qkv):
    rows, part = held_one.shape[1], held_one.shape[2] // 2

    def in_order(pieces):
        bit = 1
        while bit < G:
            on = (index[0] & bit) != 0
            pieces = [jnp.where(on, pieces[i ^ bit], pieces[i]) for i in range(G)]
            bit *= 2
        return pieces

    for side, one, two in ((0, held_one, held_two), (1, got_one, got_two)):
        mine = index[2] if side == 0 else 1 - index[2]
        where = pl.ds(pl.multiple_of(mine * rows, rows), rows)
        ones = [one[k].astype(F32) for k in range(G)]
        for k in range(G):
            out[where, k * part : (k + 1) * part] = ones[k][:, :part]
        for i, piece in enumerate(in_order([p[:, part:] for p in ones])):
            qkv[where, (2 * G + i) * part : (2 * G + i + 1) * part] = piece
        mine = index[1] if side == 0 else 1 - index[1]
        where = pl.ds(pl.multiple_of(mine * rows, rows), rows)
        for i, piece in enumerate(in_order([two[k].astype(F32) for k in range(G)])):
            for j in range(2):
                qkv[where, (j * G + i) * part : (j * G + i + 1) * part] = piece[
                    :, j * part : (j + 1) * part
                ]


def norm_parts(value):
    centre = value - jnp.mean(value, axis=-1, keepdims=True)
    spread = jnp.mean(centre * centre, axis=-1, keepdims=True)
    scale = lax.rsqrt(spread + EPS)
    return centre * scale, scale


def norm_back(upstream, hat, scale, gain):
    scaled = upstream * gain
    first = jnp.mean(scaled, axis=-1, keepdims=True)
    second = jnp.mean(scaled * hat, axis=-1, keepdims=True)
    return scale * (scaled - first - hat * second)


def on_device(
    replicas,
    tokens,
    segment_ids,
    cotangent,
    qkv_weight,
    qv_bias,
    out_weight,
    out_bias,
    norm1_gain,
    norm1_shift,
    up_weight,
    up_bias,
    down_weight,
    down_bias,
    norm2_gain,
    norm2_shift,
):
    place = lax.axis_index("group")
    me = lax.axis_index("replica")
    rows, width = tokens.shape[1], tokens.shape[2]
    part = width // G
    hidden = up_weight.shape[1] // G
    heads = part // HD
    bits = list(range(replicas.bit_length() - 1))
    first_y = bits
    first_z = [1, 0] + bits[2:]
    index = jnp.stack([place, me & 1, (me >> 1) & 1]).astype(jnp.int32)

    own_x = tokens[0]
    x_blocks = gather_rows(own_x)
    block = jax.ShapeDtypeStruct((part, 3 * part), BF)
    qkv_rows = call(pack_kernel, [block] * G, [index, qkv_weight])
    qkv_rows = [qkv_rows[0]] + [gx(qkv_rows[k], k) for k in range(1, G)]
    smalls = (qv_bias, out_bias, norm1_gain, norm1_shift, down_bias, norm2_gain, norm2_shift)
    smalls = after(smalls, qkv_rows[1], x_blocks[1])
    small = jnp.concatenate(smalls).reshape(1, -1)
    small = jnp.concatenate(xor_order(list(gather_rows(small)), place), axis=0).astype(F32)
    qv = small[:, : 2 * part].reshape(2, width)
    vectors = small[:, 2 * part :].reshape(G, 6, part).transpose(1, 0, 2).reshape(6, width)
    out_b, gain1, shift1, down_b, gain2, shift2 = [vectors[i] for i in range(6)]
    up_bias = up_bias.astype(F32)
    qkv_local = jnp.concatenate(xor_order(qkv_rows, place), axis=0)
    qkv_local, up_weight = lax.optimization_barrier((qkv_local, up_weight))
    up_rows = [
        lax.dynamic_slice_in_dim(up_weight, (place ^ k) * hidden, hidden, 1) for k in range(G)
    ]
    up_rows = [up_rows[0]] + [gx(up_rows[k], k) for k in range(1, G)]
    own_qv = lax.dynamic_slice_in_dim(qv, place * part, part, 1)
    bias = jnp.concatenate([own_qv[0], jnp.zeros((part,), F32), own_qv[1]])
    segs = segment_ids.reshape(G, rows)
    segs = jnp.concatenate(
        [lax.dynamic_index_in_dim(segs, place ^ k, 0, keepdims=False) for k in range(G)]
    )
    same = segs[:, None] == segs[None, :]

    x_all = jnp.concatenate(x_blocks, axis=0)
    proj = (dot(x_all, qkv_local) + bias).astype(BF)
    scale = HD**-0.5
    attended, kept = [], []
    for h in range(heads):
        q = proj[:, h * HD : (h + 1) * HD]
        k = proj[:, part + h * HD : part + (h + 1) * HD]
        v = proj[:, 2 * part + h * HD : 2 * part + (h + 1) * HD]
        scores = jnp.where(same, dot_t(q, k) * scale, jnp.float32(-1e30))
        peak = jnp.max(scores, axis=-1, keepdims=True)
        expo = jnp.exp(scores - peak)
        probs = expo / jnp.sum(expo, axis=-1, keepdims=True)
        low = probs.astype(BF)
        attended.append(dot(low, v).astype(BF))
        kept.append((q, k, v, probs, low))
    attended = jnp.concatenate(attended, axis=1)
    branch, up_rows = lax.optimization_barrier((dot(attended, out_weight), up_rows))
    up_local = jnp.concatenate(xor_order(up_rows, place), axis=0)
    branch = scatter_rows([branch[k * rows : (k + 1) * rows] for k in range(G)])
    first = own_x.astype(F32) + branch + out_b
    hat1, scale1 = norm_parts(first)
    normed = hat1 * gain1 + shift1
    normed_low = jnp.concatenate(gather_rows(normed.astype(BF)), axis=0)
    pre = dot(normed_low, up_local) + up_bias
    cdf = 0.5 * (1.0 + lax.erf(pre * (0.5**0.5)))
    act = (pre * cdf).astype(BF)
    slope = cdf + pre * jnp.exp(-0.5 * pre * pre) * ((2 * jnp.pi) ** -0.5)
    second = dot(act, down_weight)
    second = scatter_rows([second[k * rows : (k + 1) * rows] for k in range(G)])
    hat2, scale2 = norm_parts(normed + second + down_b)
    output = (hat2 * gain2 + shift2).astype(BF)

    up_stream = cotangent[0].astype(F32)
    d_sum = norm_back(up_stream, hat2, scale2, gain2)
    d_second = d_sum.astype(BF)
    vec_gain2 = jnp.sum(up_stream * hat2, axis=0)
    vec_shift2 = jnp.sum(up_stream, axis=0)
    vec_down = jnp.sum(d_second.astype(F32), axis=0)
    d_second_all = jnp.concatenate(gather_rows(d_second), axis=0)
    down = Scatter(t_dot(act, d_second_all).astype(BF)[None], first_y, me, replicas)
    down_got = down.swap(down.send())
    d_pre = (dot_t(d_second_all, down_weight) * slope).astype(BF)
    vec_up = jnp.sum(d_pre.astype(F32), axis=0)
    d_normed = dot_t(d_pre, up_local)
    far = d_normed[2 * rows : 3 * rows] + gx(d_normed[3 * rows :].astype(BF), 1).astype(F32)
    far = far.astype(BF)
    near = gx(d_normed[rows : 2 * rows].astype(BF), 1)
    grad_up = t_dot(normed_low, after(d_pre, far)).astype(BF).reshape(G, part, hidden)
    up = Scatter(grad_up, first_z, me, replicas)
    up_got = up.swap(up.send())
    d_normed = d_sum + d_normed[:rows] + near.astype(F32) + gx(far, 2).astype(F32)

    d_first = norm_back(d_normed, hat1, scale1, gain1)
    vec_gain1 = jnp.sum(d_normed * hat1, axis=0)
    vec_shift1 = jnp.sum(d_normed, axis=0)
    d_branch = d_first.astype(BF)
    vec_out = jnp.sum(d_branch.astype(F32), axis=0)
    d_branch_blocks = gather_rows(d_branch)
    d_branch_all = jnp.concatenate(d_branch_blocks, axis=0)
    down_got = down.step(after(down_got, d_branch_blocks[2]))
    up_got = up.step(after(up_got, d_branch_blocks[2]))
    grad_out = t_dot(attended, d_branch_all).astype(BF)
    grad_out = grad_out.reshape(part, G, part).transpose(1, 0, 2)
    d_att = dot_t(d_branch_all, out_weight).astype(BF)
    d_q, d_k, d_v = [], [], []
    for h in range(heads):
        q, k, v, probs, low = kept[h]
        d_o = d_att[:, h * HD : (h + 1) * HD]
        d_v.append(t_dot(low, d_o).astype(BF))
        d_probs = dot_t(d_o, v)
        inner = jnp.sum(probs * d_probs, axis=-1, keepdims=True)
        d_scores = (probs * (d_probs - inner)).astype(BF)
        d_q.append((dot(d_scores, k) * scale).astype(BF))
        d_k.append((t_dot(d_scores, q) * scale).astype(BF))
    d_v = jnp.concatenate(d_v, axis=1)
    d_qk = jnp.concatenate(d_q + d_k, axis=1)
    grad_v = t_dot(x_all, d_v).astype(BF).reshape(G, part, part)
    one = Scatter(jnp.concatenate([grad_out, grad_v], axis=2), first_z, me, replicas)
    one_send = one.send()
    grad_qk = t_dot(x_all, d_qk).astype(BF).reshape(G, part, 2 * part)
    two = Scatter(grad_qk, first_y, me, replicas)
    two_send = two.send()

    one_got, two_got = one.swap(one_send), two.swap(two_send)
    down_got = down.step(after(down_got, two_send))
    up_got = up.step(after(up_got, two_send))
    d_proj = jnp.concatenate([after(d_qk, two_send), d_v], axis=1)
    sums = jnp.sum(d_proj.astype(F32), axis=0)
    d_in = dot_t(d_proj, qkv_local)
    far = d_in[2 * rows : 3 * rows] + gx(d_in[3 * rows :].astype(BF), 1).astype(F32)
    near = gx(d_in[rows : 2 * rows].astype(BF), 1)
    vecs = jnp.concatenate(
        [
            jnp.stack([vec_out, vec_gain1, vec_shift1, vec_down, vec_gain2, vec_shift2]).reshape(-1),
            lax.dynamic_update_slice_in_dim(jnp.zeros((G * hidden,), F32), vec_up, place * hidden, 0),
            lax.dynamic_update_slice_in_dim(
                jnp.zeros((3, width), F32), sums.reshape(3, part), place * part, 1
            ).reshape(-1),
        ]
    ).reshape(-1, width)
    vecs = vecs + gx(vecs, 1)

    one_got, two_got = one.step(one_got), two.step(two_got)
    far = gx(after(far.astype(BF), two_got), 2)
    d_in = d_first + d_in[:rows] + near.astype(F32) + far.astype(F32)
    grad_tokens = d_in.astype(BF)
    vecs = vecs + gx(after(vecs, two_got), 2)
    down_piece = down.piece(after(down_got, one_got, two_got))
    up_piece = up.piece(after(up_got, one_got, two_got))

    one_got, two_got = one.step(one_got), two.step(two_got)

    def outgoing(pieces):
        return [lax.dynamic_index_in_dim(pieces, place ^ k, 0, keepdims=False) for k in range(G)]

    def exchange(pieces):
        return jnp.stack([pieces[0]] + [gx(pieces[k], k) for k in range(1, G)])

    down = Gather(after(down_piece, two_send), first_y, me, replicas)
    down_got = down.swap()
    up_piece = exchange(outgoing(up_piece))
    vecs = vecs + rx(vecs, 1, replicas)

    one_piece, two_piece = one.piece(one_got), two.piece(two_got)
    mine = jnp.concatenate([one_piece[:, :, part:], two_piece], axis=2)
    mine = outgoing(mine)
    qkv_piece = exchange(mine)
    up = Gather(after(up_piece, mine), first_z, me, replicas)
    up_got = up.swap()
    down_got = down.step(after(down_got, mine))
    vecs = vecs + rx(after(vecs, mine), 2, replicas)

    one = Gather(
        jnp.concatenate([one_piece[:, :, :part], qkv_piece[:, :, :part]], axis=2),
        first_z,
        me,
        replicas,
    )
    two = Gather(qkv_piece[:, :, part:], first_y, me, replicas)
    one_got, two_got = one.swap(), two.swap()
    up_got = up.step(after(up_got, one.value))
    down_got = down.step(after(down_got, one.value))
    for bit in bits[2:]:
        vecs = vecs + rx(after(vecs, one.value), 1 << bit, replicas)

    while len(one.left) > 1:
        one_got, two_got = one.step(one_got), two.step(two_got)
        if len(up.left) > 1:
            up_got = up.step(after(up_got, one.value))
        while len(down.left) > 1:
            down_got = down.step(after(down_got, one.value))
    while len(up.left) > 1:
        up_got = up.step(up_got)
    grad_down = call(
        join_kernel,
        jax.ShapeDtypeStruct((hidden, width), F32),
        [index, down.value[0], after(down_got, one.value)[0]],
    )
    grad_up = call(
        join_up_kernel,
        jax.ShapeDtypeStruct((part, G * hidden), F32),
        [index, up.value, after(up_got, one.value)],
    )
    grad_out, grad_qkv = call(
        join_tail_kernel,
        [
            jax.ShapeDtypeStruct((part, width), F32),
            jax.ShapeDtypeStruct((part, 3 * width), F32),
        ],
        [index, one.value, one_got, two.value, two_got],
    )

    six = lax.dynamic_slice_in_dim(vecs[:6], place * part, part, 1)
    vec_up = lax.dynamic_slice_in_dim(vecs[6 : 6 + G].reshape(-1), place * hidden, hidden, 0)
    qvs = jnp.concatenate([vecs[6 + G], vecs[8 + G]])
    vec_qv = lax.dynamic_slice_in_dim(qvs, place * 2 * part, 2 * part, 0)
    return (
        output[None],
        grad_tokens[None],
        grad_qkv,
        vec_qv,
        grad_out,
        six[0],
        six[1],
        six[2],
        grad_up,
        vec_up,
        grad_down,
        six[3],
        six[4],
        six[5],
    )


def solution(mesh):
    rows = P("replica", "group", None)
    flat = P("group")
    matrix = P("group", None)
    in_specs = (
        rows,
        P("replica", None),
        rows,
        matrix,
        flat,
        matrix,
        flat,
        flat,
        flat,
        matrix,
        flat,
        matrix,
        flat,
        flat,
        flat,
    )
    out_specs = (
        rows,
        rows,
        matrix,
        flat,
        matrix,
        flat,
        flat,
        flat,
        matrix,
        flat,
        matrix,
        flat,
        flat,
        flat,
    )
    return jax.shard_map(
        partial(on_device, mesh.shape["replica"]),
        mesh=mesh,
        in_specs=in_specs,
        out_specs=out_specs,
        check_vma=False,
    )
```

```python
from functools import partial

import jax
import jax.numpy as jnp
from jax import lax
from jax.experimental import pallas as pl
from jax.experimental.pallas import tpu as pltpu
from jax.sharding import PartitionSpec as P

HD = 64
G = 4
EPS = 1e-05
VECS = 16
BF = jnp.bfloat16
F32 = jnp.float32


def gx(value, bits):
    return lax.ppermute(value, "group", [(i, i ^ bits) for i in range(G)])


def rx(value, bits, count):
    return lax.ppermute(value, "replica", [(i, i ^ bits) for i in range(count)])


def dot(a, b):
    return jnp.dot(a, b, preferred_element_type=F32)


def dot_t(a, b):
    return lax.dot_general(a, b, (((1,), (1,)), ((), ())), preferred_element_type=F32)


def t_dot(a, b):
    return lax.dot_general(a, b, (((0,), (0,)), ((), ())), preferred_element_type=F32)


def xor_order(items, place):
    count = len(items)
    bit = 1
    while bit < count:
        on = (place & bit) != 0
        items = [jnp.where(on, items[i ^ bit], items[i]) for i in range(count)]
        bit *= 2
    return items


def gather_rows(own):
    far = gx(own, 2)
    near = gx(own, 1)
    return own, near, far, gx(far, 1)


def scatter_rows(parts):
    far = parts[2] + gx(parts[3].astype(BF), 1).astype(F32)
    far = gx(far.astype(BF), 2)
    near = gx(parts[1].astype(BF), 1)
    return parts[0] + near.astype(F32) + far.astype(F32)


def after(value, *others):
    return lax.optimization_barrier((value, others))[0]


class Scatter:
    def __init__(self, value, order, me, count):
        self.held, self.rows = [(value, 0)], value.shape[1]
        self.left, self.me, self.count = list(order), me, count

    def total(self, side):
        cut = [
            lax.dynamic_slice_in_dim(array, start + side * self.rows, self.rows, 1).astype(F32)
            for array, start in self.held
        ]
        return sum(cut[1:], cut[0])

    def begin(self):
        self.rows //= 2
        self.mine = (self.me >> self.left[0]) & 1

    def send(self):
        self.begin()
        self.sent = self.total(1 - self.mine).astype(BF)
        return self.sent

    def swap(self, half):
        return rx(half, 1 << self.left.pop(0), self.count)

    def take(self, got):
        moved = [(array, start + self.mine * self.rows) for array, start in self.held]
        self.held = moved + [(got, 0)]

    def step(self, got):
        self.take(got)
        return self.swap(self.send())

    def piece(self, got):
        self.take(got)
        return self.total(0).astype(BF)


class Gather:
    def __init__(self, value, order, me, count, vecs=None):
        self.value, self.left, self.me, self.count = value, list(order), me, count
        self.vecs = vecs

    def swap(self):
        sent = self.value
        if self.vecs is not None:
            sent = sent.reshape(-1, sent.shape[2])
            sent = jnp.concatenate([sent, self.vecs.astype(BF)], axis=0)
        return rx(sent, 1 << self.left[-1], self.count)

    def take(self, got):
        if self.vecs is not None:
            blocks, rows, columns = self.value.shape
            self.vecs = self.vecs + got[blocks * rows :].astype(F32)
            got = got[: blocks * rows].reshape(blocks, rows, columns)
        on = ((self.me >> self.left.pop()) & 1) != 0
        self.value = jnp.concatenate(
            [jnp.where(on, got, self.value), jnp.where(on, self.value, got)], axis=1
        )

    def step(self, got):
        self.take(got)
        return self.swap()


def whole_spec():
    return pl.BlockSpec(memory_space=pltpu.VMEM)


def index_spec():
    return pl.BlockSpec(memory_space=pltpu.SMEM)


def call(kernel, out_shape, inputs):
    single = not isinstance(out_shape, (list, tuple))
    outs = [out_shape] if single else list(out_shape)
    got = pl.pallas_call(
        kernel,
        out_shape=outs,
        in_specs=[index_spec()] + [whole_spec()] * (len(inputs) - 1),
        out_specs=[whole_spec()] * len(outs),
        compiler_params=pltpu.CompilerParams(vmem_limit_bytes=48 * 1024 * 1024),
        cost_estimate=pl.CostEstimate(flops=0, bytes_accessed=0, transcendentals=0),
    )(*inputs)
    return got[0] if single else got


def pack_kernel(index, weight, *sends):
    part = weight.shape[0]
    for own in range(G):

        @pl.when(index[0] == own)
        def _():
            for k in range(G):
                dest = own ^ k
                for j in range(3):
                    start = (j * G + dest) * part
                    sends[k][:, j * part : (j + 1) * part] = weight[:, start : start + part]


def join_kernel(index, held, got, out):
    rows = held.shape[0]
    mine = index[1]
    out[pl.ds(pl.multiple_of(mine * rows, rows), rows), :] = held[...].astype(F32)
    out[pl.ds(pl.multiple_of((1 - mine) * rows, rows), rows), :] = got[...].astype(F32)


def join_up_kernel(index, held, got, out):
    rows, columns = held.shape[1], held.shape[2]
    mine = index[2]
    for k in range(G):
        where = pl.ds(pl.multiple_of((index[0] ^ k) * columns, columns), columns)
        out[pl.ds(pl.multiple_of(mine * rows, rows), rows), where] = held[k].astype(F32)
        out[pl.ds(pl.multiple_of((1 - mine) * rows, rows), rows), where] = got[k].astype(F32)


def join_tail_kernel(index, held_one, got_one, held_two, got_two, vecs, out, qkv, sums):
    rows, part = held_one.shape[1], held_one.shape[2] // 2

    def in_order(pieces):
        bit = 1
        while bit < G:
            on = (index[0] & bit) != 0
            pieces = [jnp.where(on, pieces[i ^ bit], pieces[i]) for i in range(G)]
            bit *= 2
        return pieces

    for side, one, two in ((0, held_one, held_two), (1, got_one, got_two)):
        mine = index[2] if side == 0 else 1 - index[2]
        where = pl.ds(pl.multiple_of(mine * rows, rows), rows)
        ones = [one[k].astype(F32) for k in range(G)]
        for k in range(G):
            out[where, k * part : (k + 1) * part] = ones[k][:, :part]
        for i, piece in enumerate(in_order([p[:, part:] for p in ones])):
            qkv[where, (2 * G + i) * part : (2 * G + i + 1) * part] = piece
        mine = index[1] if side == 0 else 1 - index[1]
        where = pl.ds(pl.multiple_of(mine * rows, rows), rows)
        if side == 0:
            twos = [two[k].astype(F32) for k in range(G)]
        else:
            twos = [two[k * rows : (k + 1) * rows, :].astype(F32) for k in range(G)]
        for i, piece in enumerate(in_order(twos)):
            for j in range(2):
                qkv[where, (j * G + i) * part : (j * G + i + 1) * part] = piece[
                    :, j * part : (j + 1) * part
                ]
    sums[...] = vecs[...] + got_two[G * held_two.shape[1] :, :].astype(F32)


def attention_back_kernel(index, d_branch, out_weight, proj, lse, seg_key, seg_query, attended, x, *outs):
    d_qk, d_v, one, two, one_send, two_send = outs
    part = out_weight.shape[0]
    scale = HD**-0.5
    d_att = dot_t(out_weight[...], d_branch[...]).astype(BF)
    same = seg_key[...] == seg_query[...]
    for h in range(part // HD):
        at = h * HD
        q = proj[at : at + HD, :]
        k = proj[part + at : part + at + HD, :]
        v = proj[2 * part + at : 2 * part + at + HD, :]
        d_o = d_att[at : at + HD, :]
        scores = jnp.where(same, t_dot(k, q) * scale, jnp.float32(-1e30))
        probs = jnp.exp(scores - lse[h : h + 1, :])
        d_probs = t_dot(v, d_o)
        inner = jnp.sum(probs * d_probs, axis=0, keepdims=True)
        d_scores = (probs * (d_probs - inner)).astype(BF)
        d_v[at : at + HD, :] = dot_t(d_o, probs.astype(BF)).astype(BF)
        d_qk[at : at + HD, :] = (dot(k, d_scores) * scale).astype(BF)
        d_qk[part + at : part + at + HD, :] = (dot_t(q, d_scores) * scale).astype(BF)
    grad_out = dot(attended[...], d_branch[...])
    grad_v = dot_t(x[...], d_v[...])
    grad_qk = dot_t(x[...], d_qk[...])
    for i in range(G):
        where = slice(i * part, (i + 1) * part)
        one[i] = jnp.concatenate([grad_out[:, where], grad_v[where, :]], axis=1).astype(BF)
        two[i] = grad_qk[where, :].astype(BF)
    keep = part // 2
    one_side = pl.ds(pl.multiple_of((1 - index[2]) * keep, keep), keep)
    two_side = pl.ds(pl.multiple_of((1 - index[1]) * keep, keep), keep)
    for i in range(G):
        one_send[i] = one[i, one_side, :]
        two_send[i] = two[i, two_side, :]


def input_grad_kernel(index, d_qk, d_v, weight, *refs):
    vectors, (near, far_send, own, far, vecs) = refs[:7], refs[7:]
    rows, width = own.shape
    part, total = d_v.shape
    for block, out in enumerate((own, near, far, far_send)):
        where = pl.ds(block * rows, rows)
        value = lax.dot_general(
            d_qk[:, where],
            weight[:, : 2 * part],
            (((0,), (1,)), ((), ())),
            preferred_element_type=F32,
        )
        value += lax.dot_general(
            d_v[:, where],
            weight[:, 2 * part :],
            (((0,), (1,)), ((), ())),
            preferred_element_type=F32,
        )
        if block == 3:
            out[:rows, :] = value.astype(BF)
        else:
            out[...] = value.astype(out.dtype)
    ones = jnp.ones((8, total), BF)
    sums = dot_t(ones, d_qk[...])[:1]
    sums = [sums[:, :part], sums[:, part:], dot_t(ones, d_v[...])[:1]]
    lines = [vector[...] for vector in vectors[:6]]
    lines += [jnp.where(index[0] == i, vectors[6][...], 0.0) for i in range(G)]
    for j in range(3):
        lines.append(
            jnp.concatenate([jnp.where(index[0] == i, sums[j], 0.0) for i in range(G)], axis=1)
        )
    lines.append(jnp.zeros((VECS - len(lines), width), F32))
    value = jnp.concatenate(lines, axis=0)
    vecs[...] = value
    far_send[rows:, :] = value.astype(BF)


def add_two_kernel(index, far, vecs, got, far_out, vecs_out):
    rows = far.shape[0]
    far_out[:rows, :] = (far[...] + got[:rows, :].astype(F32)).astype(BF)
    value = vecs[...] + got[rows:, :].astype(F32)
    vecs_out[...] = value
    far_out[rows:, :] = value.astype(BF)


def norm_parts(value):
    centre = value - jnp.mean(value, axis=-1, keepdims=True)
    spread = jnp.mean(centre * centre, axis=-1, keepdims=True)
    scale = lax.rsqrt(spread + EPS)
    return centre * scale, scale


def norm_back(upstream, hat, scale, gain):
    scaled = upstream * gain
    first = jnp.mean(scaled, axis=-1, keepdims=True)
    second = jnp.mean(scaled * hat, axis=-1, keepdims=True)
    return scale * (scaled - first - hat * second)


def on_device(
    replicas,
    tokens,
    segment_ids,
    cotangent,
    qkv_weight,
    qv_bias,
    out_weight,
    out_bias,
    norm1_gain,
    norm1_shift,
    up_weight,
    up_bias,
    down_weight,
    down_bias,
    norm2_gain,
    norm2_shift,
):
    place = lax.axis_index("group")
    me = lax.axis_index("replica")
    rows, width = tokens.shape[1], tokens.shape[2]
    part = width // G
    hidden = up_weight.shape[1] // G
    heads = part // HD
    bits = list(range(replicas.bit_length() - 1))
    first_y = bits
    first_z = [1, 0] + bits[2:]
    index = jnp.stack([place, me & 1, (me >> 1) & 1]).astype(jnp.int32)

    own_x = tokens[0]
    x_blocks = gather_rows(own_x)
    block = jax.ShapeDtypeStruct((part, 3 * part), BF)
    qkv_rows = call(pack_kernel, [block] * G, [index, qkv_weight])
    qkv_rows = [qkv_rows[0]] + [gx(qkv_rows[k], k) for k in range(1, G)]
    smalls = (qv_bias, out_bias, norm1_gain, norm1_shift, down_bias, norm2_gain, norm2_shift)
    smalls = after(smalls, qkv_rows[1], x_blocks[1])
    small = jnp.concatenate(smalls).reshape(1, -1)
    small_all = jnp.concatenate(xor_order(list(gather_rows(small)), place), axis=0).astype(F32)
    qv = small_all[:, : 2 * part].reshape(2, width)
    vectors = small_all[:, 2 * part :].reshape(G, 6, part).transpose(1, 0, 2).reshape(6, width)
    out_b, gain1, shift1, down_b, gain2, shift2 = [vectors[i] for i in range(6)]
    up_bias = up_bias.astype(F32)
    qkv_local = jnp.concatenate(xor_order(qkv_rows, place), axis=0)
    up_weight = after(up_weight, small)
    up_rows = [
        lax.dynamic_slice_in_dim(up_weight, (place ^ k) * hidden, hidden, 1) for k in range(G)
    ]
    qkv_local = after(qkv_local, up_rows)
    up_rows = [up_rows[0]] + [gx(up_rows[k], k) for k in range(1, G)]
    own_qv = lax.dynamic_slice_in_dim(qv, place * part, part, 1)
    bias = jnp.concatenate([own_qv[0], jnp.zeros((part,), F32), own_qv[1]])
    segs = segment_ids.reshape(G, rows)
    segs = jnp.concatenate(
        [lax.dynamic_index_in_dim(segs, place ^ k, 0, keepdims=False) for k in range(G)]
    )
    same = segs[:, None] == segs[None, :]

    x_all = jnp.concatenate(x_blocks, axis=0)
    proj = (dot(x_all, qkv_local) + bias).astype(BF)
    scale = HD**-0.5
    attended, lse = [], []
    for h in range(heads):
        q = proj[:, h * HD : (h + 1) * HD]
        k = proj[:, part + h * HD : part + (h + 1) * HD]
        v = proj[:, 2 * part + h * HD : 2 * part + (h + 1) * HD]
        scores = jnp.where(same, dot_t(q, k) * scale, jnp.float32(-1e30))
        peak = jnp.max(scores, axis=-1, keepdims=True)
        expo = jnp.exp(scores - peak)
        total = jnp.sum(expo, axis=-1, keepdims=True)
        attended.append(dot((expo / total).astype(BF), v).astype(BF))
        lse.append((peak + jnp.log(total)).reshape(1, -1))
    attended = jnp.concatenate(attended, axis=1)
    branch, up_rows = lax.optimization_barrier((dot(attended, out_weight), up_rows))
    up_local = jnp.concatenate(xor_order(up_rows, place), axis=0)
    branch = scatter_rows([branch[k * rows : (k + 1) * rows] for k in range(G)])
    first = own_x.astype(F32) + branch + out_b
    hat1, scale1 = norm_parts(first)
    normed = hat1 * gain1 + shift1
    normed_low = jnp.concatenate(gather_rows(after(normed.astype(BF), up_local)), axis=0)
    pre = dot(normed_low, up_local) + up_bias
    cdf = 0.5 * (1.0 + lax.erf(pre * (0.5**0.5)))
    act = (pre * cdf).astype(BF)
    slope = cdf + pre * jnp.exp(-0.5 * pre * pre) * ((2 * jnp.pi) ** -0.5)
    second = dot(act, down_weight)
    second = scatter_rows([second[k * rows : (k + 1) * rows] for k in range(G)])
    hat2, scale2 = norm_parts(normed + second + down_b)
    output = (hat2 * gain2 + shift2).astype(BF)

    up_stream = cotangent[0].astype(F32)
    d_sum = norm_back(up_stream, hat2, scale2, gain2)
    d_second = d_sum.astype(BF)
    vec_gain2 = jnp.sum(up_stream * hat2, axis=0, keepdims=True)
    vec_shift2 = jnp.sum(up_stream, axis=0, keepdims=True)
    vec_down = jnp.sum(d_second.astype(F32), axis=0, keepdims=True)
    d_second_all = jnp.concatenate(gather_rows(d_second), axis=0)
    down = Scatter(t_dot(act, d_second_all).astype(BF)[None], first_y, me, replicas)
    down_got = down.swap(down.send())
    d_pre = (dot_t(d_second_all, down_weight) * slope).astype(BF)
    vec_up = jnp.sum(d_pre.astype(F32), axis=0, keepdims=True)
    d_normed = dot_t(d_pre, up_local)
    far = d_normed[2 * rows : 3 * rows] + gx(d_normed[3 * rows :].astype(BF), 1).astype(F32)
    far = far.astype(BF)
    near = gx(d_normed[rows : 2 * rows].astype(BF), 1)
    grad_up = t_dot(normed_low, after(d_pre, far)).astype(BF).reshape(G, part, hidden)
    up = Scatter(grad_up, first_z, me, replicas)
    up_got = up.swap(up.send())
    d_normed = d_sum + d_normed[:rows] + near.astype(F32) + gx(far, 2).astype(F32)

    d_first = norm_back(d_normed, hat1, scale1, gain1)
    vec_gain1 = jnp.sum(d_normed * hat1, axis=0, keepdims=True)
    vec_shift1 = jnp.sum(d_normed, axis=0, keepdims=True)
    d_branch = d_first.astype(BF)
    vec_out = jnp.sum(d_branch.astype(F32), axis=0, keepdims=True)
    d_branch_blocks = gather_rows(d_branch)
    d_branch_all = jnp.concatenate(d_branch_blocks, axis=0)
    down_got = down.step(after(down_got, d_branch_blocks[2]))
    up_got = up.step(after(up_got, d_branch_blocks[2]))
    half = jax.ShapeDtypeStruct((G, part // 2, 2 * part), BF)
    d_qk, d_v, grad_one, grad_two, one_send, two_send = call(
        attention_back_kernel,
        [
            jax.ShapeDtypeStruct((2 * part, G * rows), BF),
            jax.ShapeDtypeStruct((part, G * rows), BF),
            jax.ShapeDtypeStruct((G, part, 2 * part), BF),
            jax.ShapeDtypeStruct((G, part, 2 * part), BF),
            half,
            half,
        ],
        [
            index,
            after(d_branch_all, down.sent, up.sent),
            out_weight,
            proj.T,
            jnp.concatenate(lse),
            segs.reshape(-1, 1),
            segs.reshape(1, -1),
            attended.T,
            x_all.T,
        ],
    )
    one = Scatter(grad_one, first_z, me, replicas)
    two = Scatter(grad_two, first_y, me, replicas)
    one.begin()
    two.begin()

    one_got, two_got = one.swap(one_send), two.swap(two_send)
    down_got = down.step(after(down_got, two_send))
    up_got = up.step(after(up_got, two_send))
    vectors = [vec_out, vec_gain1, vec_shift1, vec_down, vec_gain2, vec_shift2, vec_up]
    near, far_send, own, far, vecs = call(
        input_grad_kernel,
        [
            jax.ShapeDtypeStruct((rows, width), BF),
            jax.ShapeDtypeStruct((rows + VECS, width), BF),
            jax.ShapeDtypeStruct((rows, width), F32),
            jax.ShapeDtypeStruct((rows, width), F32),
            jax.ShapeDtypeStruct((VECS, width), F32),
        ],
        [index, d_qk, d_v, qkv_local]
        + vectors,
    )
    near, far_got = gx(near, 1), gx(far_send, 1)
    one_got, two_got = after((one_got, two_got), down.sent, up.sent)

    one_got, two_got = one.step(one_got), two.step(two_got)
    far, vecs = call(
        add_two_kernel,
        [
            jax.ShapeDtypeStruct((rows + VECS, width), BF),
            jax.ShapeDtypeStruct((VECS, width), F32),
        ],
        [index, far, vecs, after(far_got, two_got)],
    )
    far = gx(far, 2)
    down_piece = down.piece(after(down_got, one_got, two_got))
    up_piece = up.piece(after(up_got, one_got, two_got))

    one_got, two_got = one.step(one_got), two.step(two_got)

    def outgoing(pieces):
        return [lax.dynamic_index_in_dim(pieces, place ^ k, 0, keepdims=False) for k in range(G)]

    def exchange(pieces):
        return jnp.stack([pieces[0]] + [gx(pieces[k], k) for k in range(1, G)])

    down = Gather(after(down_piece, two_send), first_y, me, replicas)
    down_got = down.swap()
    up_piece = exchange(outgoing(up_piece))
    one_got, two_got = after((one_got, two_got), far)

    one_piece, two_piece = one.piece(one_got), two.piece(two_got)
    mine = jnp.concatenate([one_piece[:, :, part:], two_piece], axis=2)
    mine = outgoing(mine)
    qkv_piece = exchange(mine)
    up = Gather(after(up_piece, mine), first_z, me, replicas)
    up_got = up.swap()
    down_got = down.step(after(down_got, mine))
    vecs = vecs + far[rows:].astype(F32)
    vecs = vecs.reshape(-1, 2 * part)
    far = after(far, qkv_piece)
    grad_tokens = (d_first + own + near.astype(F32) + far[:rows].astype(F32)).astype(BF)

    one = Gather(
        jnp.concatenate([one_piece[:, :, :part], qkv_piece[:, :, :part]], axis=2),
        first_z,
        me,
        replicas,
    )
    two = Gather(qkv_piece[:, :, part:], first_y, me, replicas, vecs)
    one_got, two_got = one.swap(), two.swap()
    up_got = up.step(after(up_got, one.value))
    down_got = down.step(after(down_got, one.value))

    while len(one.left) > 1:
        one_got, two_got = one.step(one_got), two.step(two_got)
        if len(up.left) > 1:
            up_got = up.step(after(up_got, one.value))
        while len(down.left) > 1:
            down_got = down.step(after(down_got, one.value))
    while len(up.left) > 1:
        up_got = up.step(up_got)
    grad_down = call(
        join_kernel,
        jax.ShapeDtypeStruct((hidden, width), F32),
        [index, down.value[0], after(down_got, one.value)[0]],
    )
    grad_up = call(
        join_up_kernel,
        jax.ShapeDtypeStruct((part, G * hidden), F32),
        [index, up.value, after(up_got, one.value)],
    )
    one_got, two_got = after((one_got, two_got), grad_down, grad_up, grad_tokens)
    grad_out, grad_qkv, vecs = call(
        join_tail_kernel,
        [
            jax.ShapeDtypeStruct((part, width), F32),
            jax.ShapeDtypeStruct((part, 3 * width), F32),
            jax.ShapeDtypeStruct((2 * VECS, 2 * part), F32),
        ],
        [index, one.value, one_got, two.value, two_got, two.vecs],
    )
    vecs = vecs.reshape(VECS, width)

    six = lax.dynamic_slice_in_dim(vecs[:6], place * part, part, 1)
    vec_up = lax.dynamic_slice_in_dim(vecs[6 : 6 + G].reshape(-1), place * hidden, hidden, 0)
    qvs = jnp.concatenate([vecs[6 + G], vecs[8 + G]])
    vec_qv = lax.dynamic_slice_in_dim(qvs, place * 2 * part, 2 * part, 0)
    return (
        output[None],
        grad_tokens[None],
        grad_qkv,
        vec_qv,
        grad_out,
        six[0],
        six[1],
        six[2],
        grad_up,
        vec_up,
        grad_down,
        six[3],
        six[4],
        six[5],
    )


def solution(mesh):
    rows = P("replica", "group", None)
    flat = P("group")
    matrix = P("group", None)
    in_specs = (
        rows,
        P("replica", None),
        rows,
        matrix,
        flat,
        matrix,
        flat,
        flat,
        flat,
        matrix,
        flat,
        matrix,
        flat,
        flat,
        flat,
    )
    out_specs = (
        rows,
        rows,
        matrix,
        flat,
        matrix,
        flat,
        flat,
        flat,
        matrix,
        flat,
        matrix,
        flat,
        flat,
        flat,
    )
    return jax.shard_map(
        partial(on_device, mesh.shape["replica"]),
        mesh=mesh,
        in_specs=in_specs,
        out_specs=out_specs,
        check_vma=False,
    )
```

```python
from functools import partial

import jax
import jax.numpy as jnp
from jax import lax
from jax.experimental import pallas as pl
from jax.experimental.pallas import tpu as pltpu
from jax.sharding import PartitionSpec as P

HD = 64
G = 4
EPS = 1e-05
VECS = 16
BF = jnp.bfloat16
F32 = jnp.float32


def gx(value, bits):
    return lax.ppermute(value, "group", [(i, i ^ bits) for i in range(G)])


def rx(value, bits, count):
    return lax.ppermute(value, "replica", [(i, i ^ bits) for i in range(count)])


def dot(a, b):
    return jnp.dot(a, b, preferred_element_type=F32)


def dot_t(a, b):
    return lax.dot_general(a, b, (((1,), (1,)), ((), ())), preferred_element_type=F32)


def t_dot(a, b):
    return lax.dot_general(a, b, (((0,), (0,)), ((), ())), preferred_element_type=F32)


def xor_order(items, place):
    count = len(items)
    bit = 1
    while bit < count:
        on = (place & bit) != 0
        items = [jnp.where(on, items[i ^ bit], items[i]) for i in range(count)]
        bit *= 2
    return items


def gather_rows(own):
    far = gx(own, 2)
    near = gx(own, 1)
    return own, near, far, gx(far, 1)


def scatter_rows(parts):
    far = parts[2] + gx(parts[3].astype(BF), 1).astype(F32)
    far = gx(far.astype(BF), 2)
    near = gx(parts[1].astype(BF), 1)
    return parts[0] + near.astype(F32) + far.astype(F32)


def after(value, *others):
    return lax.optimization_barrier((value, others))[0]


class Scatter:
    def __init__(self, value, order, me, count):
        self.held, self.rows = [(value, 0)], value.shape[1]
        self.left, self.me, self.count = list(order), me, count

    def total(self, side):
        cut = [
            lax.dynamic_slice_in_dim(array, start + side * self.rows, self.rows, 1).astype(F32)
            for array, start in self.held
        ]
        return sum(cut[1:], cut[0])

    def begin(self):
        self.rows //= 2
        self.mine = (self.me >> self.left[0]) & 1

    def send(self):
        self.begin()
        self.sent = self.total(1 - self.mine).astype(BF)
        return self.sent

    def swap(self, half):
        return rx(half, 1 << self.left.pop(0), self.count)

    def take(self, got):
        moved = [(array, start + self.mine * self.rows) for array, start in self.held]
        self.held = moved + [(got, 0)]

    def step(self, got):
        self.take(got)
        return self.swap(self.send())

    def piece(self, got):
        self.take(got)
        return self.total(0).astype(BF)


class Gather:
    def __init__(self, value, order, me, count, vecs=None):
        self.value, self.left, self.me, self.count = value, list(order), me, count
        self.vecs = vecs

    def swap(self):
        sent = self.value
        if self.vecs is not None:
            sent = sent.reshape(-1, sent.shape[2])
            sent = jnp.concatenate([sent, self.vecs.astype(BF)], axis=0)
        return rx(sent, 1 << self.left[-1], self.count)

    def take(self, got):
        if self.vecs is not None:
            blocks, rows, columns = self.value.shape
            self.vecs = self.vecs + got[blocks * rows :].astype(F32)
            got = got[: blocks * rows].reshape(blocks, rows, columns)
        on = ((self.me >> self.left.pop()) & 1) != 0
        self.value = jnp.concatenate(
            [jnp.where(on, got, self.value), jnp.where(on, self.value, got)], axis=1
        )

    def step(self, got):
        self.take(got)
        return self.swap()


def whole_spec():
    return pl.BlockSpec(memory_space=pltpu.VMEM)


def index_spec():
    return pl.BlockSpec(memory_space=pltpu.SMEM)


def call(kernel, out_shape, inputs):
    single = not isinstance(out_shape, (list, tuple))
    outs = [out_shape] if single else list(out_shape)
    got = pl.pallas_call(
        kernel,
        out_shape=outs,
        in_specs=[index_spec()] + [whole_spec()] * (len(inputs) - 1),
        out_specs=[whole_spec()] * len(outs),
        compiler_params=pltpu.CompilerParams(vmem_limit_bytes=48 * 1024 * 1024),
        cost_estimate=pl.CostEstimate(flops=0, bytes_accessed=0, transcendentals=0),
    )(*inputs)
    return got[0] if single else got


def pack_kernel(index, weight, *sends):
    part = weight.shape[0]
    for own in range(G):

        @pl.when(index[0] == own)
        def _():
            for k in range(G):
                dest = own ^ k
                for j in range(3):
                    start = (j * G + dest) * part
                    sends[k][:, j * part : (j + 1) * part] = weight[:, start : start + part]


def join_kernel(index, held, got, out):
    rows = held.shape[0]
    mine = index[1]
    out[pl.ds(pl.multiple_of(mine * rows, rows), rows), :] = held[...].astype(F32)
    out[pl.ds(pl.multiple_of((1 - mine) * rows, rows), rows), :] = got[...].astype(F32)


def join_up_kernel(index, held, got, out):
    rows, columns = held.shape[1], held.shape[2]
    mine = index[2]
    for k in range(G):
        where = pl.ds(pl.multiple_of((index[0] ^ k) * columns, columns), columns)
        out[pl.ds(pl.multiple_of(mine * rows, rows), rows), where] = held[k].astype(F32)
        out[pl.ds(pl.multiple_of((1 - mine) * rows, rows), rows), where] = got[k].astype(F32)


def join_tail_kernel(index, held_one, got_one, held_two, got_two, vecs, out, qkv, sums):
    rows, part = held_one.shape[1], held_one.shape[2] // 2

    def in_order(pieces):
        bit = 1
        while bit < G:
            on = (index[0] & bit) != 0
            pieces = [jnp.where(on, pieces[i ^ bit], pieces[i]) for i in range(G)]
            bit *= 2
        return pieces

    for side, one, two in ((0, held_one, held_two), (1, got_one, got_two)):
        mine = index[2] if side == 0 else 1 - index[2]
        where = pl.ds(pl.multiple_of(mine * rows, rows), rows)
        ones = [one[k].astype(F32) for k in range(G)]
        for k in range(G):
            out[where, k * part : (k + 1) * part] = ones[k][:, :part]
        for i, piece in enumerate(in_order([p[:, part:] for p in ones])):
            qkv[where, (2 * G + i) * part : (2 * G + i + 1) * part] = piece
        mine = index[1] if side == 0 else 1 - index[1]
        where = pl.ds(pl.multiple_of(mine * rows, rows), rows)
        if side == 0:
            twos = [two[k].astype(F32) for k in range(G)]
        else:
            twos = [two[k * rows : (k + 1) * rows, :].astype(F32) for k in range(G)]
        for i, piece in enumerate(in_order(twos)):
            for j in range(2):
                qkv[where, (j * G + i) * part : (j * G + i + 1) * part] = piece[
                    :, j * part : (j + 1) * part
                ]
    sums[...] = vecs[...] + got_two[G * held_two.shape[1] :, :].astype(F32)


def hidden_kernel(index, own, near, far, last, up, bias, down, act, slope, *outs):
    rows = own.shape[0]
    for block, ref in enumerate((own, near, far, last)):
        where = pl.ds(block * rows, rows)
        pre = dot(ref[...], up[...]) + bias[...]
        cdf = 0.5 * (1.0 + lax.erf(pre * (0.5**0.5)))
        act[where, :] = (pre * cdf).astype(BF)
        slope[where, :] = cdf + pre * jnp.exp(-0.5 * pre * pre) * ((2 * jnp.pi) ** -0.5)
    for block, out in enumerate(outs):
        where = pl.ds(block * rows, rows)
        out[...] = dot(act[where, :], down[...]).astype(out.dtype)


def attention_back_kernel(index, d_branch, out_weight, proj, lse, seg_key, seg_query, attended, x, *outs):
    d_qk, d_v, one, two, one_send, two_send = outs
    part = out_weight.shape[0]
    scale = HD**-0.5
    d_att = dot_t(out_weight[...], d_branch[...]).astype(BF)
    same = seg_key[...] == seg_query[...]
    for h in range(part // HD):
        at = h * HD
        q = proj[at : at + HD, :]
        k = proj[part + at : part + at + HD, :]
        v = proj[2 * part + at : 2 * part + at + HD, :]
        d_o = d_att[at : at + HD, :]
        scores = jnp.where(same, t_dot(k, q) * scale, jnp.float32(-1e30))
        probs = jnp.exp(scores - lse[h : h + 1, :])
        d_probs = t_dot(v, d_o)
        inner = jnp.sum(probs * d_probs, axis=0, keepdims=True)
        d_scores = (probs * (d_probs - inner)).astype(BF)
        d_v[at : at + HD, :] = dot_t(d_o, probs.astype(BF)).astype(BF)
        d_qk[at : at + HD, :] = (dot(k, d_scores) * scale).astype(BF)
        d_qk[part + at : part + at + HD, :] = (dot_t(q, d_scores) * scale).astype(BF)
    grad_out = dot(attended[...].T, d_branch[...])
    x_turned = x[...].T
    grad_v = dot_t(x_turned, d_v[...])
    grad_qk = dot_t(x_turned, d_qk[...])
    for i in range(G):
        where = slice(i * part, (i + 1) * part)
        one[i] = jnp.concatenate([grad_out[:, where], grad_v[where, :]], axis=1).astype(BF)
        two[i] = grad_qk[where, :].astype(BF)
    keep = part // 2
    one_side = pl.ds(pl.multiple_of((1 - index[2]) * keep, keep), keep)
    two_side = pl.ds(pl.multiple_of((1 - index[1]) * keep, keep), keep)
    for i in range(G):
        one_send[i] = one[i, one_side, :]
        two_send[i] = two[i, two_side, :]


def input_grad_kernel(index, d_qk, d_v, weight, *refs):
    vectors, (near, far_send, own, far, vecs) = refs[:7], refs[7:]
    rows, width = own.shape
    part, total = d_v.shape
    for block, out in enumerate((own, near, far, far_send)):
        where = pl.ds(block * rows, rows)
        value = lax.dot_general(
            d_qk[:, where],
            weight[:, : 2 * part],
            (((0,), (1,)), ((), ())),
            preferred_element_type=F32,
        )
        value += lax.dot_general(
            d_v[:, where],
            weight[:, 2 * part :],
            (((0,), (1,)), ((), ())),
            preferred_element_type=F32,
        )
        if block == 3:
            out[:rows, :] = value.astype(BF)
        else:
            out[...] = value.astype(out.dtype)
    ones = jnp.ones((8, total), BF)
    sums = dot_t(ones, d_qk[...])[:1]
    sums = [sums[:, :part], sums[:, part:], dot_t(ones, d_v[...])[:1]]
    lines = [vector[...] for vector in vectors[:6]]
    lines += [jnp.where(index[0] == i, vectors[6][...], 0.0) for i in range(G)]
    for j in range(3):
        lines.append(
            jnp.concatenate([jnp.where(index[0] == i, sums[j], 0.0) for i in range(G)], axis=1)
        )
    lines.append(jnp.zeros((VECS - len(lines), width), F32))
    value = jnp.concatenate(lines, axis=0)
    vecs[...] = value
    far_send[rows:, :] = value.astype(BF)


def add_two_kernel(index, far, vecs, got, far_out, vecs_out):
    rows = far.shape[0]
    far_out[:rows, :] = (far[...] + got[:rows, :].astype(F32)).astype(BF)
    value = vecs[...] + got[rows:, :].astype(F32)
    vecs_out[...] = value
    far_out[rows:, :] = value.astype(BF)


def norm_parts(value):
    centre = value - jnp.mean(value, axis=-1, keepdims=True)
    spread = jnp.mean(centre * centre, axis=-1, keepdims=True)
    scale = lax.rsqrt(spread + EPS)
    return centre * scale, scale


def norm_back(upstream, hat, scale, gain):
    scaled = upstream * gain
    first = jnp.mean(scaled, axis=-1, keepdims=True)
    second = jnp.mean(scaled * hat, axis=-1, keepdims=True)
    return scale * (scaled - first - hat * second)


def on_device(
    replicas,
    tokens,
    segment_ids,
    cotangent,
    qkv_weight,
    qv_bias,
    out_weight,
    out_bias,
    norm1_gain,
    norm1_shift,
    up_weight,
    up_bias,
    down_weight,
    down_bias,
    norm2_gain,
    norm2_shift,
):
    place = lax.axis_index("group")
    me = lax.axis_index("replica")
    rows, width = tokens.shape[1], tokens.shape[2]
    part = width // G
    hidden = up_weight.shape[1] // G
    heads = part // HD
    bits = list(range(replicas.bit_length() - 1))
    first_y = bits
    first_z = [1, 0] + bits[2:]
    index = jnp.stack([place, me & 1, (me >> 1) & 1]).astype(jnp.int32)

    own_x = tokens[0]
    x_blocks = gather_rows(own_x)
    block = jax.ShapeDtypeStruct((part, 3 * part), BF)
    qkv_rows = call(pack_kernel, [block] * G, [index, qkv_weight])
    qkv_rows = [qkv_rows[0]] + [gx(qkv_rows[k], k) for k in range(1, G)]
    smalls = (qv_bias, out_bias, norm1_gain, norm1_shift, down_bias, norm2_gain, norm2_shift)
    smalls = after(smalls, qkv_rows[1], x_blocks[1])
    small = jnp.concatenate(smalls).reshape(1, -1)
    small_all = jnp.concatenate(xor_order(list(gather_rows(small)), place), axis=0).astype(F32)
    qv = small_all[:, : 2 * part].reshape(2, width)
    vectors = small_all[:, 2 * part :].reshape(G, 6, part).transpose(1, 0, 2).reshape(6, width)
    out_b, gain1, shift1, down_b, gain2, shift2 = [vectors[i] for i in range(6)]
    up_bias = up_bias.astype(F32)
    qkv_local = jnp.concatenate(xor_order(qkv_rows, place), axis=0)
    up_weight = after(up_weight, small)
    up_rows = [
        lax.dynamic_slice_in_dim(up_weight, (place ^ k) * hidden, hidden, 1) for k in range(G)
    ]
    qkv_local = after(qkv_local, up_rows)
    up_rows = [up_rows[0]] + [gx(up_rows[k], k) for k in range(1, G)]
    own_qv = lax.dynamic_slice_in_dim(qv, place * part, part, 1)
    bias = jnp.concatenate([own_qv[0], jnp.zeros((part,), F32), own_qv[1]])
    segs = segment_ids.reshape(G, rows)
    segs = jnp.concatenate(
        [lax.dynamic_index_in_dim(segs, place ^ k, 0, keepdims=False) for k in range(G)]
    )
    same = segs[:, None] == segs[None, :]

    x_all = jnp.concatenate(x_blocks, axis=0)
    proj = (dot(x_all, qkv_local) + bias).astype(BF)
    scale = HD**-0.5
    attended, lse = [], []
    for h in range(heads):
        q = proj[:, h * HD : (h + 1) * HD]
        k = proj[:, part + h * HD : part + (h + 1) * HD]
        v = proj[:, 2 * part + h * HD : 2 * part + (h + 1) * HD]
        scores = jnp.where(same, dot_t(q, k) * scale, jnp.float32(-1e30))
        peak = jnp.max(scores, axis=-1, keepdims=True)
        expo = jnp.exp(scores - peak)
        total = jnp.sum(expo, axis=-1, keepdims=True)
        attended.append(dot((expo / total).astype(BF), v).astype(BF))
        lse.append((peak + jnp.log(total)).reshape(1, -1))
    attended = jnp.concatenate(attended, axis=1)
    branch, up_rows = lax.optimization_barrier((dot(attended, out_weight), up_rows))
    up_local = jnp.concatenate(xor_order(up_rows, place), axis=0)
    branch = scatter_rows([branch[k * rows : (k + 1) * rows] for k in range(G)])
    first = own_x.astype(F32) + branch + out_b
    hat1, scale1 = norm_parts(first)
    normed = hat1 * gain1 + shift1
    normed_blocks = gather_rows(after(normed.astype(BF), up_local))
    normed_low = jnp.concatenate(normed_blocks, axis=0)
    block = jax.ShapeDtypeStruct((rows, width), F32)
    block_low = jax.ShapeDtypeStruct((rows, width), BF)
    act, slope, second, near, far, far_send = call(
        hidden_kernel,
        [
            jax.ShapeDtypeStruct((G * rows, hidden), BF),
            jax.ShapeDtypeStruct((G * rows, hidden), F32),
            block,
            block_low,
            block,
            block_low,
        ],
        [index, *normed_blocks, up_local, up_bias.reshape(1, hidden), down_weight],
    )
    far = far + gx(far_send, 1).astype(F32)
    near = gx(near, 1)
    second = second + near.astype(F32) + gx(far.astype(BF), 2).astype(F32)
    hat2, scale2 = norm_parts(normed + second + down_b)
    output = (hat2 * gain2 + shift2).astype(BF)

    up_stream = cotangent[0].astype(F32)
    d_sum = norm_back(up_stream, hat2, scale2, gain2)
    d_second = d_sum.astype(BF)
    vec_gain2 = jnp.sum(up_stream * hat2, axis=0, keepdims=True)
    vec_shift2 = jnp.sum(up_stream, axis=0, keepdims=True)
    vec_down = jnp.sum(d_second.astype(F32), axis=0, keepdims=True)
    d_second_all = jnp.concatenate(gather_rows(d_second), axis=0)
    down = Scatter(t_dot(act, d_second_all).astype(BF)[None], first_y, me, replicas)
    down_got = down.swap(down.send())
    d_pre = (dot_t(d_second_all, down_weight) * slope).astype(BF)
    vec_up = jnp.sum(d_pre.astype(F32), axis=0, keepdims=True)
    d_normed = dot_t(d_pre, up_local)
    far = d_normed[2 * rows : 3 * rows] + gx(d_normed[3 * rows :].astype(BF), 1).astype(F32)
    far = far.astype(BF)
    near = gx(d_normed[rows : 2 * rows].astype(BF), 1)
    grad_up = t_dot(normed_low, after(d_pre, far)).astype(BF).reshape(G, part, hidden)
    up = Scatter(grad_up, first_z, me, replicas)
    up_got = up.swap(up.send())
    d_normed = d_sum + d_normed[:rows] + near.astype(F32) + gx(far, 2).astype(F32)

    d_first = norm_back(d_normed, hat1, scale1, gain1)
    vec_gain1 = jnp.sum(d_normed * hat1, axis=0, keepdims=True)
    vec_shift1 = jnp.sum(d_normed, axis=0, keepdims=True)
    d_branch = d_first.astype(BF)
    vec_out = jnp.sum(d_branch.astype(F32), axis=0, keepdims=True)
    d_branch_blocks = gather_rows(d_branch)
    d_branch_all = jnp.concatenate(d_branch_blocks, axis=0)
    down_got = down.step(after(down_got, d_branch_blocks[2]))
    up_got = up.step(after(up_got, d_branch_blocks[2]))
    half = jax.ShapeDtypeStruct((G, part // 2, 2 * part), BF)
    d_qk, d_v, grad_one, grad_two, one_send, two_send = call(
        attention_back_kernel,
        [
            jax.ShapeDtypeStruct((2 * part, G * rows), BF),
            jax.ShapeDtypeStruct((part, G * rows), BF),
            jax.ShapeDtypeStruct((G, part, 2 * part), BF),
            jax.ShapeDtypeStruct((G, part, 2 * part), BF),
            half,
            half,
        ],
        [
            index,
            after(d_branch_all, down.sent, up.sent),
            out_weight,
            proj.T,
            jnp.concatenate(lse),
            segs.reshape(-1, 1),
            segs.reshape(1, -1),
            attended,
            x_all,
        ],
    )
    one = Scatter(grad_one, first_z, me, replicas)
    two = Scatter(grad_two, first_y, me, replicas)
    one.begin()
    two.begin()

    one_got, two_got = one.swap(one_send), two.swap(two_send)
    down_got = down.step(after(down_got, two_send))
    up_got = up.step(after(up_got, two_send))
    vectors = [vec_out, vec_gain1, vec_shift1, vec_down, vec_gain2, vec_shift2, vec_up]
    near, far_send, own, far, vecs = call(
        input_grad_kernel,
        [
            jax.ShapeDtypeStruct((rows, width), BF),
            jax.ShapeDtypeStruct((rows + VECS, width), BF),
            jax.ShapeDtypeStruct((rows, width), F32),
            jax.ShapeDtypeStruct((rows, width), F32),
            jax.ShapeDtypeStruct((VECS, width), F32),
        ],
        [index, d_qk, d_v, qkv_local]
        + vectors,
    )
    near, far_got = gx(near, 1), gx(far_send, 1)
    one_got, two_got = after((one_got, two_got), down.sent, up.sent)

    one_got, two_got = one.step(one_got), two.step(two_got)
    far, vecs = call(
        add_two_kernel,
        [
            jax.ShapeDtypeStruct((rows + VECS, width), BF),
            jax.ShapeDtypeStruct((VECS, width), F32),
        ],
        [index, far, vecs, after(far_got, two_got)],
    )
    far = gx(far, 2)
    up_piece = up.piece(after(up_got, one_got, two_got))

    one_got, two_got = one.step(one_got), two.step(two_got)
    down_piece = down.piece(after(down_got, one.sent, two.sent))

    def outgoing(pieces):
        return [lax.dynamic_index_in_dim(pieces, place ^ k, 0, keepdims=False) for k in range(G)]

    def exchange(pieces):
        return jnp.stack([pieces[0]] + [gx(pieces[k], k) for k in range(1, G)])

    down = Gather(down_piece, first_y, me, replicas)
    down_got = down.swap()
    up_piece = exchange(outgoing(up_piece))
    one_got, two_got = after((one_got, two_got), far)

    one_piece, two_piece = one.piece(one_got), two.piece(two_got)
    mine = jnp.concatenate([one_piece[:, :, part:], two_piece], axis=2)
    mine = outgoing(mine)
    qkv_piece = exchange(mine)
    up = Gather(after(up_piece, mine), first_z, me, replicas)
    up_got = up.swap()
    down_got = down.step(after(down_got, mine))
    vecs = vecs + far[rows:].astype(F32)
    vecs = vecs.reshape(-1, 2 * part)
    far = after(far, qkv_piece)
    grad_tokens = (d_first + own + near.astype(F32) + far[:rows].astype(F32)).astype(BF)

    one = Gather(
        jnp.concatenate([one_piece[:, :, :part], qkv_piece[:, :, :part]], axis=2),
        first_z,
        me,
        replicas,
    )
    two = Gather(qkv_piece[:, :, part:], first_y, me, replicas, vecs)
    one_got, two_got = one.swap(), two.swap()
    up_got = up.step(after(up_got, one.value))
    down_got = down.step(after(down_got, one.value))
    one_got, two_got = after((one_got, two_got), down.value)

    while len(one.left) > 1:
        one_got, two_got = one.step(one_got), two.step(two_got)
        if len(up.left) > 1:
            up_got = up.step(after(up_got, one.value))
        while len(down.left) > 1:
            down_got = down.step(after(down_got, one.value))
    while len(up.left) > 1:
        up_got = up.step(up_got)
    grad_down = call(
        join_kernel,
        jax.ShapeDtypeStruct((hidden, width), F32),
        [index, down.value[0], after(down_got, one.value)[0]],
    )
    grad_up = call(
        join_up_kernel,
        jax.ShapeDtypeStruct((part, G * hidden), F32),
        [index, up.value, after(up_got, one.value)],
    )
    one_got, two_got = after((one_got, two_got), grad_down, grad_up, grad_tokens)
    grad_out, grad_qkv, vecs = call(
        join_tail_kernel,
        [
            jax.ShapeDtypeStruct((part, width), F32),
            jax.ShapeDtypeStruct((part, 3 * width), F32),
            jax.ShapeDtypeStruct((2 * VECS, 2 * part), F32),
        ],
        [index, one.value, one_got, two.value, two_got, two.vecs],
    )
    vecs = vecs.reshape(VECS, width)

    six = lax.dynamic_slice_in_dim(vecs[:6], place * part, part, 1)
    vec_up = lax.dynamic_slice_in_dim(vecs[6 : 6 + G].reshape(-1), place * hidden, hidden, 0)
    qvs = jnp.concatenate([vecs[6 + G], vecs[8 + G]])
    vec_qv = lax.dynamic_slice_in_dim(qvs, place * 2 * part, 2 * part, 0)
    return (
        output[None],
        grad_tokens[None],
        grad_qkv,
        vec_qv,
        grad_out,
        six[0],
        six[1],
        six[2],
        grad_up,
        vec_up,
        grad_down,
        six[3],
        six[4],
        six[5],
    )


def solution(mesh):
    rows = P("replica", "group", None)
    flat = P("group")
    matrix = P("group", None)
    in_specs = (
        rows,
        P("replica", None),
        rows,
        matrix,
        flat,
        matrix,
        flat,
        flat,
        flat,
        matrix,
        flat,
        matrix,
        flat,
        flat,
        flat,
    )
    out_specs = (
        rows,
        rows,
        matrix,
        flat,
        matrix,
        flat,
        flat,
        flat,
        matrix,
        flat,
        matrix,
        flat,
        flat,
        flat,
    )
    return jax.shard_map(
        partial(on_device, mesh.shape["replica"]),
        mesh=mesh,
        in_specs=in_specs,
        out_specs=out_specs,
        check_vma=False,
    )
```

```python
from functools import partial

import jax
import jax.numpy as jnp
from jax import lax
from jax.experimental import pallas as pl
from jax.experimental.pallas import tpu as pltpu
from jax.sharding import PartitionSpec as P

HD = 64
G = 4
EPS = 1e-05
VECS = 16
BF = jnp.bfloat16
F32 = jnp.float32


def gx(value, bits):
    return lax.ppermute(value, "group", [(i, i ^ bits) for i in range(G)])


def rx(value, bits, count):
    return lax.ppermute(value, "replica", [(i, i ^ bits) for i in range(count)])


def dot(a, b):
    return jnp.dot(a, b, preferred_element_type=F32)


def dot_t(a, b):
    return lax.dot_general(a, b, (((1,), (1,)), ((), ())), preferred_element_type=F32)


def t_dot(a, b):
    return lax.dot_general(a, b, (((0,), (0,)), ((), ())), preferred_element_type=F32)


def xor_order(items, place):
    count = len(items)
    bit = 1
    while bit < count:
        on = (place & bit) != 0
        items = [jnp.where(on, items[i ^ bit], items[i]) for i in range(count)]
        bit *= 2
    return items


def gather_rows(own):
    far = gx(own, 2)
    near = gx(own, 1)
    return own, near, far, gx(far, 1)


def scatter_rows(parts):
    far = parts[2] + gx(parts[3].astype(BF), 1).astype(F32)
    far = gx(far.astype(BF), 2)
    near = gx(parts[1].astype(BF), 1)
    return parts[0] + near.astype(F32) + far.astype(F32)


def after(value, *others):
    return lax.optimization_barrier((value, others))[0]


class Scatter:
    def __init__(self, value, order, me, count):
        self.held, self.rows = [(value, 0)], value.shape[1]
        self.left, self.me, self.count = list(order), me, count

    def total(self, side):
        cut = [
            lax.dynamic_slice_in_dim(array, start + side * self.rows, self.rows, 1).astype(F32)
            for array, start in self.held
        ]
        return sum(cut[1:], cut[0])

    def begin(self):
        self.rows //= 2
        self.mine = (self.me >> self.left[0]) & 1

    def send(self):
        self.begin()
        self.sent = self.total(1 - self.mine).astype(BF)
        return self.sent

    def swap(self, half):
        return rx(half, 1 << self.left.pop(0), self.count)

    def take(self, got):
        moved = [(array, start + self.mine * self.rows) for array, start in self.held]
        self.held = moved + [(got, 0)]

    def step(self, got):
        self.take(got)
        return self.swap(self.send())

    def piece(self, got):
        self.take(got)
        return self.total(0).astype(BF)


class Gather:
    def __init__(self, value, order, me, count, vecs=None):
        self.value, self.left, self.me, self.count = value, list(order), me, count
        self.vecs = vecs

    def swap(self):
        sent = self.value
        if self.vecs is not None:
            sent = sent.reshape(-1, sent.shape[2])
            sent = jnp.concatenate([sent, self.vecs.astype(BF)], axis=0)
        return rx(sent, 1 << self.left[-1], self.count)

    def take(self, got):
        if self.vecs is not None:
            blocks, rows, columns = self.value.shape
            self.vecs = self.vecs + got[blocks * rows :].astype(F32)
            got = got[: blocks * rows].reshape(blocks, rows, columns)
        on = ((self.me >> self.left.pop()) & 1) != 0
        self.value = jnp.concatenate(
            [jnp.where(on, got, self.value), jnp.where(on, self.value, got)], axis=1
        )

    def step(self, got):
        self.take(got)
        return self.swap()


def whole_spec():
    return pl.BlockSpec(memory_space=pltpu.VMEM)


def index_spec():
    return pl.BlockSpec(memory_space=pltpu.SMEM)


def call(kernel, out_shape, inputs):
    single = not isinstance(out_shape, (list, tuple))
    outs = [out_shape] if single else list(out_shape)
    got = pl.pallas_call(
        kernel,
        out_shape=outs,
        in_specs=[index_spec()] + [whole_spec()] * (len(inputs) - 1),
        out_specs=[whole_spec()] * len(outs),
        compiler_params=pltpu.CompilerParams(vmem_limit_bytes=48 * 1024 * 1024),
        cost_estimate=pl.CostEstimate(flops=0, bytes_accessed=0, transcendentals=0),
    )(*inputs)
    return got[0] if single else got


def pack_kernel(index, weight, *sends):
    part = weight.shape[0]
    for own in range(G):

        @pl.when(index[0] == own)
        def _():
            for k in range(G):
                dest = own ^ k
                for j in range(3):
                    start = (j * G + dest) * part
                    sends[k][:, j * part : (j + 1) * part] = weight[:, start : start + part]


def join_kernel(index, held, got, out):
    rows = held.shape[0]
    mine = index[1]
    out[pl.ds(pl.multiple_of(mine * rows, rows), rows), :] = held[...].astype(F32)
    out[pl.ds(pl.multiple_of((1 - mine) * rows, rows), rows), :] = got[...].astype(F32)


def join_up_kernel(index, held, got, out):
    rows, columns = held.shape[1], held.shape[2]
    mine = index[2]
    for k in range(G):
        where = pl.ds(pl.multiple_of((index[0] ^ k) * columns, columns), columns)
        out[pl.ds(pl.multiple_of(mine * rows, rows), rows), where] = held[k].astype(F32)
        out[pl.ds(pl.multiple_of((1 - mine) * rows, rows), rows), where] = got[k].astype(F32)


def join_tail_kernel(index, held_one, got_one, held_two, got_two, vecs, out, qkv, ups, qvs, *six):
    rows, part = held_one.shape[1], held_one.shape[2] // 2

    def in_order(pieces):
        bit = 1
        while bit < G:
            on = (index[0] & bit) != 0
            pieces = [jnp.where(on, pieces[i ^ bit], pieces[i]) for i in range(G)]
            bit *= 2
        return pieces

    for side, one, two in ((0, held_one, held_two), (1, got_one, got_two)):
        mine = index[2] if side == 0 else 1 - index[2]
        where = pl.ds(pl.multiple_of(mine * rows, rows), rows)
        ones = [one[k].astype(F32) for k in range(G)]
        for k in range(G):
            out[where, k * part : (k + 1) * part] = ones[k][:, :part]
        for i, piece in enumerate(in_order([p[:, part:] for p in ones])):
            qkv[where, (2 * G + i) * part : (2 * G + i + 1) * part] = piece
        mine = index[1] if side == 0 else 1 - index[1]
        where = pl.ds(pl.multiple_of(mine * rows, rows), rows)
        if side == 0:
            twos = [two[k].astype(F32) for k in range(G)]
        else:
            twos = [two[k * rows : (k + 1) * rows, :].astype(F32) for k in range(G)]
        for i, piece in enumerate(in_order(twos)):
            for j in range(2):
                qkv[where, (j * G + i) * part : (j * G + i + 1) * part] = piece[
                    :, j * part : (j + 1) * part
                ]
    sums = vecs[...] + got_two[G * held_two.shape[1] :, :].astype(F32)
    half = 2 * part

    def own(pieces):
        value = pieces[0]
        for i in range(1, G):
            value = jnp.where(index[0] == i, pieces[i], value)
        return value

    def line(row, start, size):
        at = 2 * row + start // half
        return sums[at : at + 1, start % half : start % half + size]

    for j in range(6):
        six[j][...] = own([line(j, i * part, part) for i in range(G)]).reshape(part)
    whole = [jnp.concatenate([line(6 + i, 0, half), line(6 + i, half, half)], axis=1) for i in range(G)]
    ups[...] = own(whole).reshape(2 * half)
    row = 6 + G
    qvs[...] = own([line(row + 2 * (i // 2), (i % 2) * half, half) for i in range(G)]).reshape(half)


def hidden_kernel(index, own, near, far, last, up, bias, down, act, slope, *outs):
    rows = own.shape[0]
    for block, ref in enumerate((own, near, far, last)):
        where = pl.ds(block * rows, rows)
        pre = dot(ref[...], up[...]) + bias[...]
        cdf = 0.5 * (1.0 + lax.erf(pre * (0.5**0.5)))
        act[where, :] = (pre * cdf).astype(BF)
        slope[where, :] = cdf + pre * jnp.exp(-0.5 * pre * pre) * ((2 * jnp.pi) ** -0.5)
    for block, out in enumerate(outs):
        where = pl.ds(block * rows, rows)
        out[...] = dot(act[where, :], down[...]).astype(out.dtype)


def attention_back_kernel(index, d_branch, out_weight, proj, lse, seg_key, seg_query, attended, x, *outs):
    d_qk, d_v, one, two, one_send, two_send = outs
    part = out_weight.shape[0]
    scale = HD**-0.5
    d_att = dot_t(out_weight[...], d_branch[...]).astype(BF)
    same = seg_key[...] == seg_query[...]
    for h in range(part // HD):
        at = h * HD
        q = proj[at : at + HD, :]
        k = proj[part + at : part + at + HD, :]
        v = proj[2 * part + at : 2 * part + at + HD, :]
        d_o = d_att[at : at + HD, :]
        scores = jnp.where(same, t_dot(k, q) * scale, jnp.float32(-1e30))
        probs = jnp.exp(scores - lse[h : h + 1, :])
        d_probs = t_dot(v, d_o)
        inner = jnp.sum(probs * d_probs, axis=0, keepdims=True)
        d_scores = (probs * (d_probs - inner)).astype(BF)
        d_v[at : at + HD, :] = dot_t(d_o, probs.astype(BF)).astype(BF)
        d_qk[at : at + HD, :] = (dot(k, d_scores) * scale).astype(BF)
        d_qk[part + at : part + at + HD, :] = (dot_t(q, d_scores) * scale).astype(BF)
    grad_out = dot(attended[...].T, d_branch[...])
    x_turned = x[...].T
    grad_v = dot_t(x_turned, d_v[...])
    grad_qk = dot_t(x_turned, d_qk[...])
    for i in range(G):
        where = slice(i * part, (i + 1) * part)
        one[i] = jnp.concatenate([grad_out[:, where], grad_v[where, :]], axis=1).astype(BF)
        two[i] = grad_qk[where, :].astype(BF)
    keep = part // 2
    one_side = pl.ds(pl.multiple_of((1 - index[2]) * keep, keep), keep)
    two_side = pl.ds(pl.multiple_of((1 - index[1]) * keep, keep), keep)
    for i in range(G):
        one_send[i] = one[i, one_side, :]
        two_send[i] = two[i, two_side, :]


def input_grad_kernel(index, d_qk, d_v, weight, *refs):
    vectors, (near, far_send, own, far, vecs) = refs[:7], refs[7:]
    rows, width = own.shape
    part, total = d_v.shape
    for block, out in enumerate((own, near, far, far_send)):
        where = pl.ds(block * rows, rows)
        value = lax.dot_general(
            d_qk[:, where],
            weight[:, : 2 * part],
            (((0,), (1,)), ((), ())),
            preferred_element_type=F32,
        )
        value += lax.dot_general(
            d_v[:, where],
            weight[:, 2 * part :],
            (((0,), (1,)), ((), ())),
            preferred_element_type=F32,
        )
        if block == 3:
            out[:rows, :] = value.astype(BF)
        else:
            out[...] = value.astype(out.dtype)
    ones = jnp.ones((8, total), BF)
    sums = dot_t(ones, d_qk[...])[:1]
    sums = [sums[:, :part], sums[:, part:], dot_t(ones, d_v[...])[:1]]
    lines = [vector[...] for vector in vectors[:6]]
    lines += [jnp.where(index[0] == i, vectors[6][...], 0.0) for i in range(G)]
    for j in range(3):
        lines.append(
            jnp.concatenate([jnp.where(index[0] == i, sums[j], 0.0) for i in range(G)], axis=1)
        )
    lines.append(jnp.zeros((VECS - len(lines), width), F32))
    value = jnp.concatenate(lines, axis=0)
    vecs[...] = value
    far_send[rows:, :] = value.astype(BF)


def add_two_kernel(index, far, vecs, got, far_out, vecs_out):
    rows = far.shape[0]
    far_out[:rows, :] = (far[...] + got[:rows, :].astype(F32)).astype(BF)
    value = vecs[...] + got[rows:, :].astype(F32)
    vecs_out[...] = value
    far_out[rows:, :] = value.astype(BF)


def norm_parts(value):
    centre = value - jnp.mean(value, axis=-1, keepdims=True)
    spread = jnp.mean(centre * centre, axis=-1, keepdims=True)
    scale = lax.rsqrt(spread + EPS)
    return centre * scale, scale


def norm_back(upstream, hat, scale, gain):
    scaled = upstream * gain
    first = jnp.mean(scaled, axis=-1, keepdims=True)
    second = jnp.mean(scaled * hat, axis=-1, keepdims=True)
    return scale * (scaled - first - hat * second)


def on_device(
    replicas,
    tokens,
    segment_ids,
    cotangent,
    qkv_weight,
    qv_bias,
    out_weight,
    out_bias,
    norm1_gain,
    norm1_shift,
    up_weight,
    up_bias,
    down_weight,
    down_bias,
    norm2_gain,
    norm2_shift,
):
    place = lax.axis_index("group")
    me = lax.axis_index("replica")
    rows, width = tokens.shape[1], tokens.shape[2]
    part = width // G
    hidden = up_weight.shape[1] // G
    heads = part // HD
    bits = list(range(replicas.bit_length() - 1))
    first_y = bits
    first_z = [1, 0] + bits[2:]
    index = jnp.stack([place, me & 1, (me >> 1) & 1]).astype(jnp.int32)

    own_x = tokens[0]
    x_blocks = gather_rows(own_x)
    block = jax.ShapeDtypeStruct((part, 3 * part), BF)
    qkv_rows = call(pack_kernel, [block] * G, [index, qkv_weight])
    qkv_rows = [qkv_rows[0]] + [gx(qkv_rows[k], k) for k in range(1, G)]
    smalls = (qv_bias, out_bias, norm1_gain, norm1_shift, down_bias, norm2_gain, norm2_shift)
    smalls = after(smalls, qkv_rows[1], x_blocks[1])
    small = jnp.concatenate(smalls).reshape(1, -1)
    small_all = jnp.concatenate(xor_order(list(gather_rows(small)), place), axis=0).astype(F32)
    qv = small_all[:, : 2 * part].reshape(2, width)
    vectors = small_all[:, 2 * part :].reshape(G, 6, part).transpose(1, 0, 2).reshape(6, width)
    out_b, gain1, shift1, down_b, gain2, shift2 = [vectors[i] for i in range(6)]
    up_bias = up_bias.astype(F32)
    qkv_local = jnp.concatenate(xor_order(qkv_rows, place), axis=0)
    up_weight = after(up_weight, small)
    up_rows = [
        lax.dynamic_slice_in_dim(up_weight, (place ^ k) * hidden, hidden, 1) for k in range(G)
    ]
    qkv_local = after(qkv_local, up_rows)
    up_rows = [up_rows[0]] + [gx(up_rows[k], k) for k in range(1, G)]
    own_qv = lax.dynamic_slice_in_dim(qv, place * part, part, 1)
    bias = jnp.concatenate([own_qv[0], jnp.zeros((part,), F32), own_qv[1]])
    segs = segment_ids.reshape(G, rows)
    segs = jnp.concatenate(
        [lax.dynamic_index_in_dim(segs, place ^ k, 0, keepdims=False) for k in range(G)]
    )
    same = segs[:, None] == segs[None, :]

    x_all = jnp.concatenate(x_blocks, axis=0)
    proj = (dot(x_all, qkv_local) + bias).astype(BF)
    scale = HD**-0.5
    attended, lse = [], []
    for h in range(heads):
        q = proj[:, h * HD : (h + 1) * HD]
        k = proj[:, part + h * HD : part + (h + 1) * HD]
        v = proj[:, 2 * part + h * HD : 2 * part + (h + 1) * HD]
        scores = jnp.where(same, dot_t(q, k) * scale, jnp.float32(-1e30))
        peak = jnp.max(scores, axis=-1, keepdims=True)
        expo = jnp.exp(scores - peak)
        total = jnp.sum(expo, axis=-1, keepdims=True)
        attended.append(dot((expo / total).astype(BF), v).astype(BF))
        lse.append((peak + jnp.log(total)).reshape(1, -1))
    attended = jnp.concatenate(attended, axis=1)
    branch, up_rows = lax.optimization_barrier((dot(attended, out_weight), up_rows))
    up_local = jnp.concatenate(xor_order(up_rows, place), axis=0)
    branch = scatter_rows([branch[k * rows : (k + 1) * rows] for k in range(G)])
    first = own_x.astype(F32) + branch + out_b
    hat1, scale1 = norm_parts(first)
    normed = hat1 * gain1 + shift1
    normed_blocks = gather_rows(after(normed.astype(BF), up_local))
    normed_low = jnp.concatenate(normed_blocks, axis=0)
    block = jax.ShapeDtypeStruct((rows, width), F32)
    block_low = jax.ShapeDtypeStruct((rows, width), BF)
    act, slope, second, near, far, far_send = call(
        hidden_kernel,
        [
            jax.ShapeDtypeStruct((G * rows, hidden), BF),
            jax.ShapeDtypeStruct((G * rows, hidden), F32),
            block,
            block_low,
            block,
            block_low,
        ],
        [index, *normed_blocks, up_local, up_bias.reshape(1, hidden), down_weight],
    )
    far = far + gx(far_send, 1).astype(F32)
    near = gx(near, 1)
    second = second + near.astype(F32) + gx(far.astype(BF), 2).astype(F32)
    hat2, scale2 = norm_parts(normed + second + down_b)
    output = (hat2 * gain2 + shift2).astype(BF)

    up_stream = cotangent[0].astype(F32)
    d_sum = norm_back(up_stream, hat2, scale2, gain2)
    d_second = d_sum.astype(BF)
    vec_gain2 = jnp.sum(up_stream * hat2, axis=0, keepdims=True)
    vec_shift2 = jnp.sum(up_stream, axis=0, keepdims=True)
    vec_down = jnp.sum(d_second.astype(F32), axis=0, keepdims=True)
    d_second_all = jnp.concatenate(gather_rows(d_second), axis=0)
    down = Scatter(t_dot(act, d_second_all).astype(BF)[None], first_y, me, replicas)
    down_got = down.swap(down.send())
    d_pre = (dot_t(d_second_all, down_weight) * slope).astype(BF)
    vec_up = jnp.sum(d_pre.astype(F32), axis=0, keepdims=True)
    d_normed = dot_t(d_pre, up_local)
    far = d_normed[2 * rows : 3 * rows] + gx(d_normed[3 * rows :].astype(BF), 1).astype(F32)
    far = far.astype(BF)
    near = gx(d_normed[rows : 2 * rows].astype(BF), 1)
    grad_up = t_dot(normed_low, after(d_pre, far)).astype(BF).reshape(G, part, hidden)
    up = Scatter(grad_up, first_z, me, replicas)
    up_got = up.swap(up.send())
    d_normed = d_sum + d_normed[:rows] + near.astype(F32) + gx(far, 2).astype(F32)

    d_first = norm_back(d_normed, hat1, scale1, gain1)
    vec_gain1 = jnp.sum(d_normed * hat1, axis=0, keepdims=True)
    vec_shift1 = jnp.sum(d_normed, axis=0, keepdims=True)
    d_branch = d_first.astype(BF)
    vec_out = jnp.sum(d_branch.astype(F32), axis=0, keepdims=True)
    d_branch_blocks = gather_rows(d_branch)
    d_branch_all = jnp.concatenate(d_branch_blocks, axis=0)
    down_got = down.step(after(down_got, d_branch_blocks[2]))
    up_got = up.step(after(up_got, d_branch_blocks[2]))
    half = jax.ShapeDtypeStruct((G, part // 2, 2 * part), BF)
    d_qk, d_v, grad_one, grad_two, one_send, two_send = call(
        attention_back_kernel,
        [
            jax.ShapeDtypeStruct((2 * part, G * rows), BF),
            jax.ShapeDtypeStruct((part, G * rows), BF),
            jax.ShapeDtypeStruct((G, part, 2 * part), BF),
            jax.ShapeDtypeStruct((G, part, 2 * part), BF),
            half,
            half,
        ],
        [
            index,
            after(d_branch_all, down.sent, up.sent),
            out_weight,
            proj.T,
            jnp.concatenate(lse),
            segs.reshape(-1, 1),
            segs.reshape(1, -1),
            attended,
            x_all,
        ],
    )
    one = Scatter(grad_one, first_z, me, replicas)
    two = Scatter(grad_two, first_y, me, replicas)
    one.begin()
    two.begin()

    one_got, two_got = one.swap(one_send), two.swap(two_send)
    down_got = down.step(after(down_got, two_send))
    up_got = up.step(after(up_got, two_send))
    vectors = [vec_out, vec_gain1, vec_shift1, vec_down, vec_gain2, vec_shift2, vec_up]
    near, far_send, own, far, vecs = call(
        input_grad_kernel,
        [
            jax.ShapeDtypeStruct((rows, width), BF),
            jax.ShapeDtypeStruct((rows + VECS, width), BF),
            jax.ShapeDtypeStruct((rows, width), F32),
            jax.ShapeDtypeStruct((rows, width), F32),
            jax.ShapeDtypeStruct((VECS, width), F32),
        ],
        [index, d_qk, d_v, qkv_local]
        + vectors,
    )
    near, far_got = gx(near, 1), gx(far_send, 1)
    one_got, two_got = after((one_got, two_got), down.sent, up.sent)

    one_got, two_got = one.step(one_got), two.step(two_got)
    far, vecs = call(
        add_two_kernel,
        [
            jax.ShapeDtypeStruct((rows + VECS, width), BF),
            jax.ShapeDtypeStruct((VECS, width), F32),
        ],
        [index, far, vecs, after(far_got, two_got)],
    )
    far = gx(far, 2)
    up_piece = up.piece(after(up_got, one_got, two_got))

    one_got, two_got = one.step(one_got), two.step(two_got)
    down_piece = down.piece(after(down_got, one.sent, two.sent))

    def outgoing(pieces):
        return [lax.dynamic_index_in_dim(pieces, place ^ k, 0, keepdims=False) for k in range(G)]

    def exchange(pieces):
        return jnp.stack([pieces[0]] + [gx(pieces[k], k) for k in range(1, G)])

    down = Gather(down_piece, first_y, me, replicas)
    down_got = down.swap()
    up_piece = exchange(outgoing(up_piece))
    one_got, two_got = after((one_got, two_got), far)

    one_piece, two_piece = one.piece(one_got), two.piece(two_got)
    mine = jnp.concatenate([one_piece[:, :, part:], two_piece], axis=2)
    mine = outgoing(mine)
    qkv_piece = exchange(mine)
    up = Gather(after(up_piece, mine), first_z, me, replicas)
    up_got = up.swap()
    down_got = down.step(after(down_got, mine))
    vecs = vecs + far[rows:].astype(F32)
    vecs = vecs.reshape(-1, 2 * part)
    far = after(far, qkv_piece)
    grad_tokens = (d_first + own + near.astype(F32) + far[:rows].astype(F32)).astype(BF)

    one = Gather(
        jnp.concatenate([one_piece[:, :, :part], qkv_piece[:, :, :part]], axis=2),
        first_z,
        me,
        replicas,
    )
    two = Gather(qkv_piece[:, :, part:], first_y, me, replicas, vecs)
    one_got, two_got = one.swap(), two.swap()
    up_got = up.step(after(up_got, one.value))
    down_got = down.step(after(down_got, one.value))
    one_got, two_got = after((one_got, two_got), down.value)

    while len(one.left) > 1:
        one_got, two_got = one.step(one_got), two.step(two_got)
        if len(up.left) > 1:
            up_got = up.step(after(up_got, one.value))
        while len(down.left) > 1:
            down_got = down.step(after(down_got, one.value))
    while len(up.left) > 1:
        up_got = up.step(up_got)
    grad_down = call(
        join_kernel,
        jax.ShapeDtypeStruct((hidden, width), F32),
        [index, down.value[0], after(down_got, one.value)[0]],
    )
    grad_up = call(
        join_up_kernel,
        jax.ShapeDtypeStruct((part, G * hidden), F32),
        [index, up.value, after(up_got, one.value)],
    )
    one_got, two_got = after((one_got, two_got), grad_down, grad_up, grad_tokens)
    grad_out, grad_qkv, vec_up, vec_qv, *six = call(
        join_tail_kernel,
        [
            jax.ShapeDtypeStruct((part, width), F32),
            jax.ShapeDtypeStruct((part, 3 * width), F32),
            jax.ShapeDtypeStruct((hidden,), F32),
            jax.ShapeDtypeStruct((2 * part,), F32),
        ]
        + [jax.ShapeDtypeStruct((part,), F32)] * 6,
        [index, one.value, one_got, two.value, two_got, two.vecs],
    )

    return (
        output[None],
        grad_tokens[None],
        grad_qkv,
        vec_qv,
        grad_out,
        six[0],
        six[1],
        six[2],
        grad_up,
        vec_up,
        grad_down,
        six[3],
        six[4],
        six[5],
    )


def solution(mesh):
    rows = P("replica", "group", None)
    flat = P("group")
    matrix = P("group", None)
    in_specs = (
        rows,
        P("replica", None),
        rows,
        matrix,
        flat,
        matrix,
        flat,
        flat,
        flat,
        matrix,
        flat,
        matrix,
        flat,
        flat,
        flat,
    )
    out_specs = (
        rows,
        rows,
        matrix,
        flat,
        matrix,
        flat,
        flat,
        flat,
        matrix,
        flat,
        matrix,
        flat,
        flat,
        flat,
    )
    return jax.shard_map(
        partial(on_device, mesh.shape["replica"]),
        mesh=mesh,
        in_specs=in_specs,
        out_specs=out_specs,
        check_vma=False,
    )
```

```python
from functools import partial

import jax
import jax.numpy as jnp
from jax import lax
from jax.experimental import pallas as pl
from jax.experimental.pallas import tpu as pltpu
from jax.sharding import PartitionSpec as P

HD = 64
G = 4
EPS = 1e-05
VECS = 16
BF = jnp.bfloat16
F32 = jnp.float32


def gx(value, bits):
    return lax.ppermute(value, "group", [(i, i ^ bits) for i in range(G)])


def rx(value, bits, count):
    return lax.ppermute(value, "replica", [(i, i ^ bits) for i in range(count)])


def dot(a, b):
    return jnp.dot(a, b, preferred_element_type=F32)


def dot_t(a, b):
    return lax.dot_general(a, b, (((1,), (1,)), ((), ())), preferred_element_type=F32)


def t_dot(a, b):
    return lax.dot_general(a, b, (((0,), (0,)), ((), ())), preferred_element_type=F32)


def xor_order(items, place):
    count = len(items)
    bit = 1
    while bit < count:
        on = (place & bit) != 0
        items = [jnp.where(on, items[i ^ bit], items[i]) for i in range(count)]
        bit *= 2
    return items


def gather_rows(own):
    far = gx(own, 2)
    near = gx(own, 1)
    return own, near, far, gx(far, 1)


def scatter_rows(parts):
    far = parts[2] + gx(parts[3].astype(BF), 1).astype(F32)
    far = gx(far.astype(BF), 2)
    near = gx(parts[1].astype(BF), 1)
    return parts[0] + near.astype(F32) + far.astype(F32)


def after(value, *others):
    return lax.optimization_barrier((value, others))[0]


class Scatter:
    def __init__(self, value, order, me, count):
        self.held, self.rows = [(value, 0)], value.shape[1]
        self.left, self.me, self.count = list(order), me, count

    def total(self, side):
        cut = [
            lax.dynamic_slice_in_dim(array, start + side * self.rows, self.rows, 1).astype(F32)
            for array, start in self.held
        ]
        return sum(cut[1:], cut[0])

    def begin(self):
        self.rows //= 2
        self.mine = (self.me >> self.left[0]) & 1

    def send(self):
        self.begin()
        self.sent = self.total(1 - self.mine).astype(BF)
        return self.sent

    def swap(self, half):
        return rx(half, 1 << self.left.pop(0), self.count)

    def take(self, got):
        moved = [(array, start + self.mine * self.rows) for array, start in self.held]
        self.held = moved + [(got, 0)]

    def step(self, got):
        self.take(got)
        return self.swap(self.send())

    def piece(self, got):
        self.take(got)
        return self.total(0).astype(BF)


class Gather:
    def __init__(self, value, order, me, count, vecs=None):
        self.value, self.left, self.me, self.count = value, list(order), me, count
        self.vecs = vecs

    def swap(self):
        sent = self.value
        if self.vecs is not None:
            sent = sent.reshape(-1, sent.shape[2])
            sent = jnp.concatenate([sent, self.vecs.astype(BF)], axis=0)
        return rx(sent, 1 << self.left[-1], self.count)

    def take(self, got):
        if self.vecs is not None:
            blocks, rows, columns = self.value.shape
            self.vecs = self.vecs + got[blocks * rows :].astype(F32)
            got = got[: blocks * rows].reshape(blocks, rows, columns)
        on = ((self.me >> self.left.pop()) & 1) != 0
        self.value = jnp.concatenate(
            [jnp.where(on, got, self.value), jnp.where(on, self.value, got)], axis=1
        )

    def step(self, got):
        self.take(got)
        return self.swap()


def whole_spec():
    return pl.BlockSpec(memory_space=pltpu.VMEM)


def index_spec():
    return pl.BlockSpec(memory_space=pltpu.SMEM)


def call(kernel, out_shape, inputs):
    single = not isinstance(out_shape, (list, tuple))
    outs = [out_shape] if single else list(out_shape)
    got = pl.pallas_call(
        kernel,
        out_shape=outs,
        in_specs=[index_spec()] + [whole_spec()] * (len(inputs) - 1),
        out_specs=[whole_spec()] * len(outs),
        compiler_params=pltpu.CompilerParams(vmem_limit_bytes=48 * 1024 * 1024),
        cost_estimate=pl.CostEstimate(flops=0, bytes_accessed=0, transcendentals=0),
    )(*inputs)
    return got[0] if single else got


def pack_kernel(index, weight, *sends):
    part = weight.shape[0]
    for own in range(G):

        @pl.when(index[0] == own)
        def _():
            for k in range(G):
                dest = own ^ k
                for j in range(3):
                    start = (j * G + dest) * part
                    sends[k][:, j * part : (j + 1) * part] = weight[:, start : start + part]


def join_kernel(index, held, got, out):
    rows = held.shape[0]
    mine = index[1]
    out[pl.ds(pl.multiple_of(mine * rows, rows), rows), :] = held[...].astype(F32)
    out[pl.ds(pl.multiple_of((1 - mine) * rows, rows), rows), :] = got[...].astype(F32)


def join_up_kernel(index, held, got, out):
    rows, columns = held.shape[1], held.shape[2]
    mine = index[2]
    for k in range(G):
        where = pl.ds(pl.multiple_of((index[0] ^ k) * columns, columns), columns)
        out[pl.ds(pl.multiple_of(mine * rows, rows), rows), where] = held[k].astype(F32)
        out[pl.ds(pl.multiple_of((1 - mine) * rows, rows), rows), where] = got[k].astype(F32)


def join_tail_kernel(index, held_one, got_one, held_two, got_two, vecs, out, qkv, ups, qvs, *six):
    rows, part = held_one.shape[1], held_one.shape[2] // 2

    def in_order(pieces):
        bit = 1
        while bit < G:
            on = (index[0] & bit) != 0
            pieces = [jnp.where(on, pieces[i ^ bit], pieces[i]) for i in range(G)]
            bit *= 2
        return pieces

    for side, one, two in ((0, held_one, held_two), (1, got_one, got_two)):
        mine = index[2] if side == 0 else 1 - index[2]
        where = pl.ds(pl.multiple_of(mine * rows, rows), rows)
        ones = [one[k].astype(F32) for k in range(G)]
        for k in range(G):
            out[where, k * part : (k + 1) * part] = ones[k][:, :part]
        for i, piece in enumerate(in_order([p[:, part:] for p in ones])):
            qkv[where, (2 * G + i) * part : (2 * G + i + 1) * part] = piece
        mine = index[1] if side == 0 else 1 - index[1]
        where = pl.ds(pl.multiple_of(mine * rows, rows), rows)
        if side == 0:
            twos = [two[k].astype(F32) for k in range(G)]
        else:
            twos = [two[k * rows : (k + 1) * rows, :].astype(F32) for k in range(G)]
        for i, piece in enumerate(in_order(twos)):
            for j in range(2):
                qkv[where, (j * G + i) * part : (j * G + i + 1) * part] = piece[
                    :, j * part : (j + 1) * part
                ]
    sums = vecs[...] + got_two[G * held_two.shape[1] :, :].astype(F32)
    half = 2 * part

    def own(pieces):
        value = pieces[0]
        for i in range(1, G):
            value = jnp.where(index[0] == i, pieces[i], value)
        return value

    def line(row, start, size):
        at = 2 * row + start // half
        return sums[at : at + 1, start % half : start % half + size]

    for j in range(6):
        six[j][...] = own([line(j, i * part, part) for i in range(G)]).reshape(part)
    whole = [jnp.concatenate([line(6 + i, 0, half), line(6 + i, half, half)], axis=1) for i in range(G)]
    ups[...] = own(whole).reshape(2 * half)
    row = 6 + G
    qvs[...] = own([line(row + 2 * (i // 2), (i % 2) * half, half) for i in range(G)]).reshape(half)


def hidden_kernel(index, own, near, far, last, up, bias, down, act, slope, *outs):
    rows = own.shape[0]
    for block, ref in enumerate((own, near, far, last)):
        where = pl.ds(block * rows, rows)
        pre = dot(ref[...], up[...]) + bias[...]
        cdf = 0.5 * (1.0 + lax.erf(pre * (0.5**0.5)))
        act[where, :] = (pre * cdf).astype(BF)
        value = cdf + pre * jnp.exp(-0.5 * pre * pre) * ((2 * jnp.pi) ** -0.5)
        slope[where, :] = value.astype(BF)
    for block, out in enumerate(outs):
        where = pl.ds(block * rows, rows)
        out[...] = dot(act[where, :], down[...]).astype(out.dtype)


def attention_back_kernel(index, d_branch, out_weight, proj, lse, seg_key, seg_query, attended, x, *outs):
    d_qk, d_v, one, two, one_send, two_send = outs
    part = out_weight.shape[0]
    scale = HD**-0.5
    d_att = dot_t(out_weight[...], d_branch[...]).astype(BF)
    same = seg_key[...] == seg_query[...]
    for h in range(part // HD):
        at = h * HD
        q = proj[at : at + HD, :]
        k = proj[part + at : part + at + HD, :]
        v = proj[2 * part + at : 2 * part + at + HD, :]
        d_o = d_att[at : at + HD, :]
        scores = jnp.where(same, t_dot(k, q) * scale, jnp.float32(-1e30))
        probs = jnp.exp(scores - lse[h : h + 1, :])
        d_probs = t_dot(v, d_o)
        inner = jnp.sum(probs * d_probs, axis=0, keepdims=True)
        d_scores = (probs * (d_probs - inner)).astype(BF)
        d_v[at : at + HD, :] = dot_t(d_o, probs.astype(BF)).astype(BF)
        d_qk[at : at + HD, :] = (dot(k, d_scores) * scale).astype(BF)
        d_qk[part + at : part + at + HD, :] = (dot_t(q, d_scores) * scale).astype(BF)
    grad_out = dot(attended[...].T, d_branch[...])
    x_turned = x[...].T
    grad_v = dot_t(x_turned, d_v[...])
    grad_qk = dot_t(x_turned, d_qk[...])
    for i in range(G):
        where = slice(i * part, (i + 1) * part)
        one[i] = jnp.concatenate([grad_out[:, where], grad_v[where, :]], axis=1).astype(BF)
        two[i] = grad_qk[where, :].astype(BF)
    keep = part // 2
    one_side = pl.ds(pl.multiple_of((1 - index[2]) * keep, keep), keep)
    two_side = pl.ds(pl.multiple_of((1 - index[1]) * keep, keep), keep)
    for i in range(G):
        one_send[i] = one[i, one_side, :]
        two_send[i] = two[i, two_side, :]


def input_grad_kernel(index, d_qk, d_v, weight, *refs):
    vectors, (near, far_send, own, far, vecs) = refs[:7], refs[7:]
    rows, width = own.shape
    part, total = d_v.shape
    for block, out in enumerate((own, near, far, far_send)):
        where = pl.ds(block * rows, rows)
        value = lax.dot_general(
            d_qk[:, where],
            weight[:, : 2 * part],
            (((0,), (1,)), ((), ())),
            preferred_element_type=F32,
        )
        value += lax.dot_general(
            d_v[:, where],
            weight[:, 2 * part :],
            (((0,), (1,)), ((), ())),
            preferred_element_type=F32,
        )
        if block == 3:
            out[:rows, :] = value.astype(BF)
        else:
            out[...] = value.astype(out.dtype)
    ones = jnp.ones((8, total), BF)
    sums = dot_t(ones, d_qk[...])[:1]
    sums = [sums[:, :part], sums[:, part:], dot_t(ones, d_v[...])[:1]]
    lines = [vector[...] for vector in vectors[:6]]
    lines += [jnp.where(index[0] == i, vectors[6][...], 0.0) for i in range(G)]
    for j in range(3):
        lines.append(
            jnp.concatenate([jnp.where(index[0] == i, sums[j], 0.0) for i in range(G)], axis=1)
        )
    lines.append(jnp.zeros((VECS - len(lines), width), F32))
    value = jnp.concatenate(lines, axis=0)
    vecs[...] = value
    far_send[rows:, :] = value.astype(BF)


def add_two_kernel(index, far, vecs, got, far_out, vecs_out):
    rows = far.shape[0]
    far_out[:rows, :] = (far[...] + got[:rows, :].astype(F32)).astype(BF)
    value = vecs[...] + got[rows:, :].astype(F32)
    vecs_out[...] = value
    far_out[rows:, :] = value.astype(BF)


def norm_parts(value):
    centre = value - jnp.mean(value, axis=-1, keepdims=True)
    spread = jnp.mean(centre * centre, axis=-1, keepdims=True)
    scale = lax.rsqrt(spread + EPS)
    return centre * scale, scale


def norm_back(upstream, hat, scale, gain):
    scaled = upstream * gain
    first = jnp.mean(scaled, axis=-1, keepdims=True)
    second = jnp.mean(scaled * hat, axis=-1, keepdims=True)
    return scale * (scaled - first - hat * second)


def on_device(
    replicas,
    tokens,
    segment_ids,
    cotangent,
    qkv_weight,
    qv_bias,
    out_weight,
    out_bias,
    norm1_gain,
    norm1_shift,
    up_weight,
    up_bias,
    down_weight,
    down_bias,
    norm2_gain,
    norm2_shift,
):
    place = lax.axis_index("group")
    me = lax.axis_index("replica")
    rows, width = tokens.shape[1], tokens.shape[2]
    part = width // G
    hidden = up_weight.shape[1] // G
    heads = part // HD
    bits = list(range(replicas.bit_length() - 1))
    first_y = bits
    first_z = [1, 0] + bits[2:]
    index = jnp.stack([place, me & 1, (me >> 1) & 1]).astype(jnp.int32)

    own_x = tokens[0]
    x_blocks = gather_rows(own_x)
    block = jax.ShapeDtypeStruct((part, 3 * part), BF)
    qkv_rows = call(pack_kernel, [block] * G, [index, qkv_weight])
    qkv_rows = [qkv_rows[0]] + [gx(qkv_rows[k], k) for k in range(1, G)]
    smalls = (qv_bias, out_bias, norm1_gain, norm1_shift, down_bias, norm2_gain, norm2_shift)
    smalls = after(smalls, qkv_rows[1], x_blocks[1])
    small = jnp.concatenate(smalls).reshape(1, -1)
    small_all = jnp.concatenate(xor_order(list(gather_rows(small)), place), axis=0).astype(F32)
    qv = small_all[:, : 2 * part].reshape(2, width)
    vectors = small_all[:, 2 * part :].reshape(G, 6, part).transpose(1, 0, 2).reshape(6, width)
    out_b, gain1, shift1, down_b, gain2, shift2 = [vectors[i] for i in range(6)]
    up_bias = up_bias.astype(F32)
    qkv_local = jnp.concatenate(xor_order(qkv_rows, place), axis=0)
    up_weight = after(up_weight, small)
    up_rows = [
        lax.dynamic_slice_in_dim(up_weight, (place ^ k) * hidden, hidden, 1) for k in range(G)
    ]
    qkv_local = after(qkv_local, up_rows)
    up_rows = [up_rows[0]] + [gx(up_rows[k], k) for k in range(1, G)]
    own_qv = lax.dynamic_slice_in_dim(qv, place * part, part, 1)
    bias = jnp.concatenate([own_qv[0], jnp.zeros((part,), F32), own_qv[1]])
    segs = segment_ids.reshape(G, rows)
    segs = jnp.concatenate(
        [lax.dynamic_index_in_dim(segs, place ^ k, 0, keepdims=False) for k in range(G)]
    )
    same = segs[:, None] == segs[None, :]

    x_all = jnp.concatenate(x_blocks, axis=0)
    proj = (dot(x_all, qkv_local) + bias).astype(BF)
    scale = HD**-0.5
    attended, lse = [], []
    for h in range(heads):
        q = proj[:, h * HD : (h + 1) * HD]
        k = proj[:, part + h * HD : part + (h + 1) * HD]
        v = proj[:, 2 * part + h * HD : 2 * part + (h + 1) * HD]
        scores = jnp.where(same, dot_t(q, k) * scale, jnp.float32(-1e30))
        peak = jnp.max(scores, axis=-1, keepdims=True)
        expo = jnp.exp(scores - peak)
        total = jnp.sum(expo, axis=-1, keepdims=True)
        attended.append(dot((expo / total).astype(BF), v).astype(BF))
        lse.append((peak + jnp.log(total)).reshape(1, -1))
    attended = jnp.concatenate(attended, axis=1)
    branch, up_rows = lax.optimization_barrier((dot(attended, out_weight), up_rows))
    up_local = jnp.concatenate(xor_order(up_rows, place), axis=0)
    branch = scatter_rows([branch[k * rows : (k + 1) * rows] for k in range(G)])
    first = own_x.astype(F32) + branch + out_b
    hat1, scale1 = norm_parts(first)
    normed = hat1 * gain1 + shift1
    normed_blocks = gather_rows(after(normed.astype(BF), up_local))
    normed_low = jnp.concatenate(normed_blocks, axis=0)
    block = jax.ShapeDtypeStruct((rows, width), F32)
    block_low = jax.ShapeDtypeStruct((rows, width), BF)
    act, slope, second, near, far, far_send = call(
        hidden_kernel,
        [
            jax.ShapeDtypeStruct((G * rows, hidden), BF),
            jax.ShapeDtypeStruct((G * rows, hidden), BF),
            block,
            block_low,
            block,
            block_low,
        ],
        [index, *normed_blocks, up_local, up_bias.reshape(1, hidden), down_weight],
    )
    far = far + gx(far_send, 1).astype(F32)
    near = gx(near, 1)
    second = second + near.astype(F32) + gx(far.astype(BF), 2).astype(F32)
    hat2, scale2 = norm_parts(normed + second + down_b)
    output = (hat2 * gain2 + shift2).astype(BF)

    up_stream = cotangent[0].astype(F32)
    d_sum = norm_back(up_stream, hat2, scale2, gain2)
    d_second = d_sum.astype(BF)
    vec_gain2 = jnp.sum(up_stream * hat2, axis=0, keepdims=True)
    vec_shift2 = jnp.sum(up_stream, axis=0, keepdims=True)
    vec_down = jnp.sum(d_second.astype(F32), axis=0, keepdims=True)
    d_second_all = jnp.concatenate(gather_rows(d_second), axis=0)
    down = Scatter(t_dot(act, d_second_all).astype(BF)[None], first_y, me, replicas)
    down_got = down.swap(down.send())
    d_pre = (dot_t(d_second_all, down_weight) * slope.astype(F32)).astype(BF)
    vec_up = jnp.sum(d_pre.astype(F32), axis=0, keepdims=True)
    d_normed = dot_t(d_pre, up_local)
    far = d_normed[2 * rows : 3 * rows] + gx(d_normed[3 * rows :].astype(BF), 1).astype(F32)
    far = far.astype(BF)
    near = gx(d_normed[rows : 2 * rows].astype(BF), 1)
    grad_up = t_dot(normed_low, after(d_pre, far)).astype(BF).reshape(G, part, hidden)
    up = Scatter(grad_up, first_z, me, replicas)
    up_got = up.swap(up.send())
    d_normed = d_sum + d_normed[:rows] + near.astype(F32) + gx(far, 2).astype(F32)

    d_first = norm_back(d_normed, hat1, scale1, gain1)
    vec_gain1 = jnp.sum(d_normed * hat1, axis=0, keepdims=True)
    vec_shift1 = jnp.sum(d_normed, axis=0, keepdims=True)
    d_branch = d_first.astype(BF)
    vec_out = jnp.sum(d_branch.astype(F32), axis=0, keepdims=True)
    d_branch_blocks = gather_rows(d_branch)
    d_branch_all = jnp.concatenate(d_branch_blocks, axis=0)
    down_got = down.step(after(down_got, d_branch_blocks[2]))
    up_got = up.step(after(up_got, d_branch_blocks[2]))
    half = jax.ShapeDtypeStruct((G, part // 2, 2 * part), BF)
    d_qk, d_v, grad_one, grad_two, one_send, two_send = call(
        attention_back_kernel,
        [
            jax.ShapeDtypeStruct((2 * part, G * rows), BF),
            jax.ShapeDtypeStruct((part, G * rows), BF),
            jax.ShapeDtypeStruct((G, part, 2 * part), BF),
            jax.ShapeDtypeStruct((G, part, 2 * part), BF),
            half,
            half,
        ],
        [
            index,
            after(d_branch_all, down.sent, up.sent),
            out_weight,
            proj.T,
            jnp.concatenate(lse),
            segs.reshape(-1, 1),
            segs.reshape(1, -1),
            attended,
            x_all,
        ],
    )
    one = Scatter(grad_one, first_z, me, replicas)
    two = Scatter(grad_two, first_y, me, replicas)
    one.begin()
    two.begin()

    one_got, two_got = one.swap(one_send), two.swap(two_send)
    down_got = down.step(after(down_got, two_send))
    up_got = up.step(after(up_got, two_send))
    vectors = [vec_out, vec_gain1, vec_shift1, vec_down, vec_gain2, vec_shift2, vec_up]
    near, far_send, own, far, vecs = call(
        input_grad_kernel,
        [
            jax.ShapeDtypeStruct((rows, width), BF),
            jax.ShapeDtypeStruct((rows + VECS, width), BF),
            jax.ShapeDtypeStruct((rows, width), F32),
            jax.ShapeDtypeStruct((rows, width), F32),
            jax.ShapeDtypeStruct((VECS, width), F32),
        ],
        [index, d_qk, d_v, qkv_local]
        + vectors,
    )
    near, far_got = gx(near, 1), gx(far_send, 1)
    one_got, two_got = after((one_got, two_got), down.sent, up.sent)

    one_got, two_got = one.step(one_got), two.step(two_got)
    far, vecs = call(
        add_two_kernel,
        [
            jax.ShapeDtypeStruct((rows + VECS, width), BF),
            jax.ShapeDtypeStruct((VECS, width), F32),
        ],
        [index, far, vecs, after(far_got, two_got)],
    )
    far = gx(far, 2)
    up_piece = up.piece(after(up_got, one_got, two_got))

    one_got, two_got = one.step(one_got), two.step(two_got)
    down_piece = down.piece(after(down_got, one.sent, two.sent))

    def outgoing(pieces):
        return [lax.dynamic_index_in_dim(pieces, place ^ k, 0, keepdims=False) for k in range(G)]

    def exchange(pieces):
        return jnp.stack([pieces[0]] + [gx(pieces[k], k) for k in range(1, G)])

    down = Gather(down_piece, first_y, me, replicas)
    down_got = down.swap()
    up_piece = exchange(outgoing(up_piece))
    one_got, two_got = after((one_got, two_got), far)

    one_piece, two_piece = one.piece(one_got), two.piece(two_got)
    mine = jnp.concatenate([one_piece[:, :, part:], two_piece], axis=2)
    mine = outgoing(mine)
    qkv_piece = exchange(mine)
    up = Gather(after(up_piece, mine), first_z, me, replicas)
    up_got = up.swap()
    down_got = down.step(after(down_got, mine))
    vecs = vecs + far[rows:].astype(F32)
    vecs = vecs.reshape(-1, 2 * part)
    far = after(far, qkv_piece)
    grad_tokens = (d_first + own + near.astype(F32) + far[:rows].astype(F32)).astype(BF)

    one = Gather(
        jnp.concatenate([one_piece[:, :, :part], qkv_piece[:, :, :part]], axis=2),
        first_z,
        me,
        replicas,
    )
    two = Gather(qkv_piece[:, :, part:], first_y, me, replicas, vecs)
    one_got, two_got = one.swap(), two.swap()
    up_got = up.step(after(up_got, one.value))
    down_got = down.step(after(down_got, one.value))
    one_got, two_got = after((one_got, two_got), down.value)

    while len(one.left) > 1:
        one_got, two_got = one.step(one_got), two.step(two_got)
        if len(up.left) > 1:
            up_got = up.step(after(up_got, one.value))
        while len(down.left) > 1:
            down_got = down.step(after(down_got, one.value))
    while len(up.left) > 1:
        up_got = up.step(up_got)
    grad_down = call(
        join_kernel,
        jax.ShapeDtypeStruct((hidden, width), F32),
        [index, down.value[0], after(down_got, one.value)[0]],
    )
    grad_up = call(
        join_up_kernel,
        jax.ShapeDtypeStruct((part, G * hidden), F32),
        [index, up.value, after(up_got, one.value)],
    )
    one_got, two_got = after((one_got, two_got), grad_down, grad_up, grad_tokens)
    grad_out, grad_qkv, vec_up, vec_qv, *six = call(
        join_tail_kernel,
        [
            jax.ShapeDtypeStruct((part, width), F32),
            jax.ShapeDtypeStruct((part, 3 * width), F32),
            jax.ShapeDtypeStruct((hidden,), F32),
            jax.ShapeDtypeStruct((2 * part,), F32),
        ]
        + [jax.ShapeDtypeStruct((part,), F32)] * 6,
        [index, one.value, one_got, two.value, two_got, two.vecs],
    )

    return (
        output[None],
        grad_tokens[None],
        grad_qkv,
        vec_qv,
        grad_out,
        six[0],
        six[1],
        six[2],
        grad_up,
        vec_up,
        grad_down,
        six[3],
        six[4],
        six[5],
    )


def solution(mesh):
    rows = P("replica", "group", None)
    flat = P("group")
    matrix = P("group", None)
    in_specs = (
        rows,
        P("replica", None),
        rows,
        matrix,
        flat,
        matrix,
        flat,
        flat,
        flat,
        matrix,
        flat,
        matrix,
        flat,
        flat,
        flat,
    )
    out_specs = (
        rows,
        rows,
        matrix,
        flat,
        matrix,
        flat,
        flat,
        flat,
        matrix,
        flat,
        matrix,
        flat,
        flat,
        flat,
    )
    return jax.shard_map(
        partial(on_device, mesh.shape["replica"]),
        mesh=mesh,
        in_specs=in_specs,
        out_specs=out_specs,
        check_vma=False,
    )
```
